32 devices in a mesh: blk: 8 (over z, x), head: 4 (over y, core).
Axes of the slice: x: 2, y: 2, z: 4, core: 2. Of those that a mesh axis runs over, the one named last changes fastest.
Arguments:
- states_in: bfloat16 [2048, 2048], P('blk'), may hold values from -12 to 12
- w_qkv: bfloat16 [3, 2048, 2048], P(None, None, 'head'), may hold values from -0.35355339 to 0.35355339
- qk_gain: float32 [2, 2048], P(None, 'head'), may hold values from 0.8 to 7.8
- w_out: bfloat16 [2048, 2048], P('head'), may hold values from -0.125 to 0.125
- post_gain: float32 [2, 2048], replicated, may hold values from 0.5 to 1.5
- w_gate_up: bfloat16 [2, 2048, 8192], P(None, None, 'blk'), may hold values from -0.125 to 0.125
- w_down: bfloat16 [8192, 2048], P('blk'), may hold values from -0.0625 to 0.0625
- cache_keys: bfloat16 [8, 256, 2048], P('blk', None, 'head'), may hold values from -6 to 6
- cache_values: bfloat16 [8, 256, 2048], P('blk', None, 'head'), may hold values from -6 to 6
- slot_node: int32 [8], replicated, may hold values from 0 to 7, each once
- node_length: int32 [8], replicated, may hold values from 1 to 256, 1280 in all
- node_parent: int32 [4], replicated, may hold values from 0 to 3
- leaf_segment: int32 [8, 256], replicated, may hold values from 0 to 7, never falling along the last dimension, each value on 1 to 128 neighbouring positions
- leaf_node: int32 [8, 8], replicated, may hold values from 4 to 7
Outputs:
- layer_out: bfloat16 [2048, 2048], P(('blk', 'head'))
The draws below stay inside these ranges and needn't reach their ends.
Inputs may be any that keep to these rules, and one draw needn't show every extreme that they name: Slot s holds node slot_node[s]; every node is held once. Rows 0 to node_length[n] - 1 of node n's slot are valid; the longest node has 256 rows. Nodes 0 to 3 are roots; middle node 4 + i hangs under root node_parent[i]. `leaf_segment`: never falls along a group; every leaf of a group has 1 to 128 tokens. `leaf_node`: every leaf hangs under a middle node.
All inputs are finite; a program needn't handle non-finite values.
Results may differ from the reference program's by a relative error of at most 0.025.
Values may be sent and summed in bfloat16 or wider, within the bound.
A program may use at most 192 MiB of HBM per device.

```python
import math
import jax
import jax.numpy as jnp
import numpy as np
from jax import lax

D = 2048
HEADS = 16
HD = 128
FF = 8192
TENANTS = 4
TOK_DEV = 256
NODE_LEN = 256
LEAVES_DEV = 8
GROUPS = 8
NODES = 8
MIDDLES = 4
TOKENS = 2048


def draw_states_in(key, part):
    key_base = jax.random.fold_in(key, 0)
    base = jax.random.truncated_normal(key_base, -6.0, 6.0, (TOKENS, D), jnp.float32)
    return base.astype(jnp.bfloat16)


def draw_w_qkv(key, part):
    key_base, key_jitter = jax.random.split(key)
    columns = HEADS * HD
    base = jax.random.truncated_normal(key_base, -6.0, 6.0, (3, D, columns), jnp.float32) / math.sqrt(D)
    column_at = jnp.arange(columns, dtype=jnp.float32) / (columns - 1)
    jitter = jnp.exp(jax.random.uniform(key_jitter, (2, 1, columns), jnp.float32, -0.35, 0.35))
    shaped = base[0:2] * (0.6 * 3.0 ** column_at) * jitter
    return jnp.concatenate([shaped, base[2:3]], axis=0).astype(jnp.bfloat16)


def draw_qk_gain(key, part):
    key_main = jax.random.fold_in(key, 0)
    columns = HEADS * HD
    return jax.random.uniform(key_main, (2, columns), jnp.float32, 0.8, 1.25)


def set_ends(drawn, own_key, low, top_value):
    spot = [jax.random.randint(jax.random.fold_in(own_key, axis), (), 0, length) for axis, length in enumerate(drawn.shape)]
    widest = drawn.shape.index(max(drawn.shape))
    beside = spot[:widest] + [(spot[widest] + 1) % drawn.shape[widest]] + spot[widest + 1:]
    return drawn.at[tuple(spot)].set(low).at[tuple(beside)].set(top_value)


def levels(own_key, shape, cuts, least, top_value):
    def one(dim, blocks):
        steps = jax.random.uniform(jax.random.fold_in(jax.random.fold_in(own_key, 6), dim), (blocks,), jnp.float32, least / len(cuts), top_value / len(cuts))
        return jnp.repeat(jnp.exp(steps), shape[dim] // blocks).reshape((-1,) + (1,) * (len(shape) - dim - 1))

    factor_of = one(*cuts[0])
    for cut in cuts[1:]:
        factor_of = factor_of * one(*cut)
    return factor_of


def length_profile(number_of, total, limit, skew):
    portions = [(1 << 20) // math.isqrt(standing ** skew) + 1 for standing in range(2, number_of + 1)]
    surplus, given = total - limit - (number_of - 1), [1] * (number_of - 1)
    while surplus > 0:
        free = [i for i in range(number_of - 1) if given[i] < limit]
        mass, remaining = sum([portions[i] for i in free]), surplus
        for i in free:
            extra = min(limit - given[i], max(1, remaining * portions[i] // mass), surplus)
            given[i] = given[i] + extra
            surplus = surplus - extra
    return np.array([limit] + given)


def uneven_parts(stream_key, amount, total, limit, skew):
    if amount == 2:
        one = jax.random.randint(stream_key, (), max(1, total - limit), min(limit, total - 1) + 1)
        return jnp.stack([one, total - one])
    sizes = jnp.asarray(length_profile(amount, total, limit, skew), jnp.int32)
    pairs = (amount - 1) // 2
    giver, sink = sizes[1:1 + 2 * pairs:2], sizes[2:2 + 2 * pairs:2]
    room = jnp.minimum(giver - 1, limit - sink)
    shifted = jax.random.randint(jax.random.fold_in(stream_key, 1), (pairs,), 0, 1 << 20) % (room + 1)
    sizes = sizes.at[1:1 + 2 * pairs:2].set(giver - shifted).at[2:2 + 2 * pairs:2].set(sink + shifted)
    return sizes[jax.random.permutation(jax.random.fold_in(stream_key, 2), amount)]


def centred(own_key, extent, width, bound, cuts=(), kind=jnp.bfloat16):
    result = jax.random.normal(own_key, extent, jnp.float32) * width
    if len(cuts) > 0:
        result = levels(own_key, extent, cuts, -0.22, 0.18) * result
    return jnp.clip(result, min=-bound, max=bound).astype(kind)


def setup_inputs(seed: int = 0) -> dict:
    key_list = jax.random.split(jax.random.key(seed), 15)
    return {
        "states_in": draw_states_in(jax.random.fold_in(key_list[14], 71), 0),
        "w_qkv": draw_w_qkv(jax.random.fold_in(key_list[14], 71), 0),
        "qk_gain": draw_qk_gain(jax.random.fold_in(key_list[14], 71), 0),
        "w_out": centred(key_list[3], (HEADS * HD, D), (HEADS * HD) ** -0.5, 0.125, ((0, 4),)),
        "post_gain": jnp.clip(1.0 + 0.1 * jax.random.normal(key_list[4], (2, D), jnp.float32), 0.5, 1.5),
        "w_gate_up": centred(key_list[5], (2, D, FF), D ** -0.5, 0.125, ((2, 8),)),
        "w_down": centred(key_list[6], (FF, D), FF ** -0.5, 0.0625, ((0, 8),)),
        "cache_keys": centred(key_list[7], (NODES, NODE_LEN, HEADS * HD), 1.0, 6.0, ((0, 8), (2, 4))),
        "cache_values": centred(key_list[8], (NODES, NODE_LEN, HEADS * HD), 1.0, 6.0, ((0, 8), (2, 4))),
        "slot_node": jax.random.permutation(key_list[9], NODES).astype(jnp.int32),
        "node_length": uneven_parts(key_list[10], NODES, NODES * NODE_LEN * 5 // 8, NODE_LEN, 1).astype(jnp.int32),
        "node_parent": set_ends(jax.random.randint(key_list[11], (MIDDLES,), 0, TENANTS), jax.random.fold_in(key_list[11], 1), 0, TENANTS - 1).astype(jnp.int32),
        "leaf_segment": jax.vmap(lambda own: jnp.searchsorted(jnp.cumsum(uneven_parts(own, LEAVES_DEV, TOK_DEV, TOK_DEV // 2, 1)), jnp.arange(TOK_DEV), side="right"))(jax.random.split(key_list[12], GROUPS)).reshape((GROUPS, TOK_DEV)).astype(jnp.int32),
        "leaf_node": set_ends(jax.random.randint(key_list[13], (GROUPS, LEAVES_DEV), TENANTS, NODES), jax.random.fold_in(key_list[13], 1), TENANTS, NODES - 1).astype(jnp.int32),
    }


EPS = 1e-06
THETA = 500000.0
NEG = -1e+30

def tree_info(leaf_segment, leaf_node, node_parent, node_length):
    groups, tok_rows = leaf_segment.shape
    leaf_count = leaf_node.shape[1]
    middles = node_parent.shape[0]
    all_nodes = node_length.shape[0]
    tenant_count = all_nodes - middles
    leaf_ids = jnp.arange(leaf_count, dtype=jnp.int32)
    onehot = (leaf_segment[:, :, None] == leaf_ids[None, None, :]).astype(jnp.int32)
    middle = lax.optimization_barrier(jnp.sum(onehot * leaf_node[:, None, :], axis=-1))
    counts = lax.optimization_barrier(jnp.sum(onehot, axis=1))
    starts = jnp.cumsum(counts, axis=1) - counts
    first_at = lax.optimization_barrier(jnp.sum(onehot * starts[:, None, :], axis=-1))
    middle_ids = jnp.arange(middles, dtype=jnp.int32) + tenant_count
    root_node = lax.optimization_barrier(jnp.sum(jnp.where(middle[..., None] == middle_ids, node_parent, 0), axis=-1))
    node_ids = jnp.arange(all_nodes, dtype=jnp.int32)
    len_middle = lax.optimization_barrier(jnp.sum(jnp.where(middle[..., None] == node_ids, node_length, 0), axis=-1))
    len_root = lax.optimization_barrier(jnp.sum(jnp.where(root_node[..., None] == node_ids, node_length, 0), axis=-1))
    offsets = jnp.arange(tok_rows, dtype=jnp.int32)[None, :] - first_at
    position = len_root + len_middle + offsets
    return (middle, root_node, position)

def rotate(values_in, position):
    half_size = values_in.shape[-1] // 2
    frequency = THETA ** (-2.0 * jnp.arange(half_size, dtype=jnp.float32) / values_in.shape[-1])
    angles = position.astype(jnp.float32)[:, None] * frequency[None, :]
    cosine = jnp.cos(angles)[:, None, :]
    sine_part = jnp.sin(angles)[:, None, :]
    lower = values_in[..., :half_size]
    upper = values_in[..., half_size:]
    return jnp.concatenate([lower * cosine - upper * sine_part, upper * cosine + lower * sine_part], axis=-1)

def rms_norm(values_in, gain):
    return values_in * lax.rsqrt(lax.optimization_barrier(jnp.mean(values_in * values_in, axis=-1, keepdims=True)) + EPS) * gain

def reference(states_in, w_qkv, qk_gain, w_out, post_gain, w_gate_up, w_down, cache_keys, cache_values, slot_node, node_length, node_parent, leaf_segment, leaf_node):
    groups, tok_rows = leaf_segment.shape
    middle, root_node, position = tree_info(leaf_segment, leaf_node, node_parent, node_length)
    qkv_raw = jnp.einsum('td,cdw->ctw', states_in.astype(jnp.float32), w_qkv.astype(jnp.float32))
    flat_position = position.reshape(-1)

    def normed(raw_part, gain):
        scaled = rms_norm(raw_part, gain)
        return rotate(scaled.reshape(-1, HEADS, HD), flat_position).astype(jnp.bfloat16)
    queries = normed(qkv_raw[0], qk_gain[0])
    keys_new = normed(qkv_raw[1], qk_gain[1])
    values_cast = qkv_raw[2].astype(jnp.bfloat16).reshape(-1, HEADS, HD)
    slots, node_rows = (cache_keys.shape[0], cache_keys.shape[1])
    flat_keys = cache_keys.reshape(slots * node_rows, HEADS, HD).astype(jnp.float32)
    flat_values = cache_values.reshape(slots * node_rows, HEADS, HD).astype(jnp.float32)
    node_ids = jnp.arange(node_length.shape[0], dtype=jnp.int32)
    slot_length = lax.optimization_barrier(jnp.sum(jnp.where(slot_node[:, None] == node_ids[None, :], node_length[None, :], 0), axis=-1))
    node_flat = jnp.broadcast_to(slot_node[:, None], (slots, node_rows)).reshape(-1)
    length_flat = jnp.broadcast_to(slot_length[:, None], (slots, node_rows)).reshape(-1)
    row_flat = jnp.broadcast_to(jnp.arange(node_rows, dtype=jnp.int32)[None, :], (slots, node_rows)).reshape(-1)
    inside = row_flat < length_flat

    def one_group(items):
        group_q, group_k, group_v, group_mid, group_root, group_seg = items
        see_cache = ((node_flat[None, :] == group_mid[:, None]) | (node_flat[None, :] == group_root[:, None])) & inside[None, :]
        order = jnp.arange(tok_rows, dtype=jnp.int32)
        see_leaf = (group_seg[:, None] == group_seg[None, :]) & (order[None, :] <= order[:, None])
        visible = jnp.concatenate([see_cache, see_leaf], axis=1)
        all_keys = jnp.concatenate([flat_keys, group_k.astype(jnp.float32)], axis=0)
        all_values = jnp.concatenate([flat_values, group_v.astype(jnp.float32)], axis=0)
        scores = jnp.einsum('rhe,khe->rhk', group_q.astype(jnp.float32), all_keys) * HD ** (-0.5)
        masked = jnp.where(visible[:, None, :], scores, NEG)
        peak = lax.optimization_barrier(jnp.max(masked, axis=-1, keepdims=True))
        weights = jnp.where(visible[:, None, :], jnp.exp(masked - peak), 0.0)
        weights_low = weights.astype(jnp.bfloat16)
        numer = jnp.einsum('rhk,khe->rhe', weights_low.astype(jnp.float32), all_values)
        return (numer / lax.optimization_barrier(jnp.sum(weights, axis=-1))[..., None]).astype(jnp.bfloat16)
    attended = lax.map(one_group, (queries.reshape(groups, tok_rows, HEADS, HD), keys_new.reshape(groups, tok_rows, HEADS, HD), values_cast.reshape(groups, tok_rows, HEADS, HD), middle, root_node, leaf_segment))
    attended = attended.reshape(groups * tok_rows, HEADS * HD)
    attn_proj = jnp.dot(attended, w_out, preferred_element_type=jnp.float32)
    mid_state = (states_in.astype(jnp.float32) + rms_norm(attn_proj, post_gain[0])).astype(jnp.bfloat16)
    gate_part = jnp.dot(mid_state, w_gate_up[0], preferred_element_type=jnp.float32)
    up_part = jnp.dot(mid_state, w_gate_up[1], preferred_element_type=jnp.float32)
    hidden = (jax.nn.silu(gate_part) * up_part).astype(jnp.bfloat16)
    mlp_proj = jnp.dot(hidden, w_down, preferred_element_type=jnp.float32)
    return (mid_state.astype(jnp.float32) + rms_norm(mlp_proj, post_gain[1])).astype(jnp.bfloat16)
```

```python
import functools

import jax
import jax.numpy as jnp
from jax import lax
from jax.experimental import pallas as pl
from jax.experimental.pallas import tpu as pltpu
from jax.sharding import PartitionSpec as P

HD = 128
EPS = 1e-06
THETA = 500000.0
NEG = -1e30
MESH = pl.DeviceIdType.MESH
BF16 = jnp.bfloat16
F32 = jnp.float32


def by_distance(at, count, step):
    back = count - 1 - at
    near = jnp.minimum(at, back)
    both = jnp.where(step % 2 == 1, at - (step + 1) // 2, at + step // 2)
    return jnp.where(step <= 2 * near, both, jnp.where(at < back, step, count - 1 - step))


def remote(src, dst, send_sem, recv_sem, **where):
    return pltpu.make_async_remote_copy(
        src_ref=src,
        dst_ref=dst,
        send_sem=send_sem,
        recv_sem=recv_sem,
        device_id=where,
        device_id_type=MESH,
    )


def meet(peers):
    barrier = pltpu.get_barrier_semaphore()
    for peer in peers:
        pl.semaphore_signal(barrier, inc=1, device_id=peer, device_id_type=MESH)
    pl.semaphore_wait(barrier, len(peers))


def mlp_kernel(
    lines,
    mid_ref, wgu_hbm, wd_hbm, gain_ref, out_ref,
    gathered, wgu, wd, hidden, whole, own_part, send_x, recv_x, send_z, recv_z,
    w_sem, g_send, g_recv, x_send, x_recv, z_send, z_recv,
):
    rows, width = mid_ref.shape
    units = wd.shape[0]
    me = lax.axis_index("blk")
    z, x = me // 2, me % 2
    other = z * 2 + 1 - x

    loads = [
        pltpu.make_async_copy(wgu_hbm.at[0], wgu.at[0], w_sem.at[0]),
        pltpu.make_async_copy(wgu_hbm.at[1], wgu.at[1], w_sem.at[1]),
        pltpu.make_async_copy(wd_hbm, wd, w_sem.at[2]),
    ]
    for load in loads:
        load.start()
    meet([{"blk": other}] + [{"blk": (z + j) % lines * 2 + x} for j in range(1, lines)])

    def block(index):
        return gathered.at[pl.ds(pl.multiple_of(index * rows, rows), rows)]

    def pass_on(index, way, target):
        return remote(block(index), block(index), g_send.at[way, index], g_recv.at[index], blk=target)

    def spread(origin, wait):
        index = origin * 2 + x
        if wait:
            pass_on(index, 0, other).wait_recv()
        pass_on(index, 0, other).start()

        @pl.when((origin <= z) & (z < lines - 1))
        def _():
            pass_on(index, 1, me + 2).start()

        @pl.when((origin >= z) & (z > 0))
        def _():
            pass_on(index, 2, me - 2).start()

    gathered[pl.ds(pl.multiple_of(me * rows, rows), rows), :] = mid_ref[...]
    spread(z, False)

    def to_x(origin):
        return remote(send_x.at[origin], recv_x.at[origin], x_send.at[origin], x_recv.at[origin], blk=other)

    def to_z(origin):
        return remote(send_z.at[origin], recv_z.at[z], z_send.at[origin], z_recv.at[z], blk=origin * 2 + x)

    def reduce_x(origin):
        to_x(origin).wait_recv()
        summed = own_part[origin] + recv_x[origin].astype(F32)
        own_part[origin] = summed
        send_z[origin] = summed.astype(BF16)

        @pl.when(origin != z)
        def _():
            to_z(origin).start()

    tile = min(256, units)
    wide = min(512, width)
    for step in range(lines):
        origin = by_distance(z, lines, step)
        if step + 1 < lines:
            spread(by_distance(z, lines, step + 1), True)
        pass_on(origin * 2 + 1 - x, 0, other).wait_recv()
        if step == 0:
            loads[0].wait()
            loads[1].wait()
        chunk = pl.ds(pl.multiple_of(origin * 2 * rows, 2 * rows), 2 * rows)

        @pl.loop(0, units // tile)
        def _(t):
            at = pl.ds(pl.multiple_of(t * tile, tile), tile)
            state = gathered[chunk, :]
            gate = jnp.dot(state, wgu[0, :, at], preferred_element_type=F32)
            up = jnp.dot(state, wgu[1, :, at], preferred_element_type=F32)
            hidden[:, at] = (gate / (1.0 + jnp.exp(-gate)) * up).astype(BF16)

        if step == 0:
            loads[2].wait()

        @pl.loop(0, width // wide)
        def _(t):
            at = pl.ds(pl.multiple_of(t * wide, wide), wide)
            whole[:, at] = jnp.dot(hidden[...], wd[:, at], preferred_element_type=F32)

        own_part[origin] = whole[pl.ds(pl.multiple_of(x * rows, rows), rows), :]
        send_x[origin] = whole[pl.ds(pl.multiple_of((1 - x) * rows, rows), rows), :].astype(BF16)
        to_x(origin).start()
        if step > 0:
            reduce_x(by_distance(z, lines, step - 1))
    reduce_x(by_distance(z, lines, lines - 1))

    total = own_part[z]
    for j in range(1, lines):
        source = (z + j) % lines
        remote(send_z.at[0], recv_z.at[source], z_send.at[0], z_recv.at[source], blk=other).wait_recv()
        total = total + recv_z[source].astype(F32)
    scale = lax.rsqrt(jnp.mean(total * total, axis=-1, keepdims=True) + EPS)
    out_ref[...] = (mid_ref[...].astype(F32) + total * scale * gain_ref[...]).astype(BF16)

    for origin in range(lines):
        index = origin * 2 + x
        to_x(origin).wait_send()
        pass_on(index, 0, other).wait_send()

        @pl.when((origin <= z) & (z < lines - 1))
        def _():
            pass_on(index, 1, me + 2).wait_send()

        @pl.when((origin >= z) & (z > 0))
        def _():
            pass_on(index, 2, me - 2).wait_send()

        @pl.when(origin != z)
        def _():
            to_z(origin).wait_send()


def mlp(mid_state, w_gate_up, w_down, gain, devices):
    rows, width = mid_state.shape
    units = w_down.shape[0]
    lines = devices // 2
    vmem = pl.BlockSpec(memory_space=pltpu.VMEM)
    hbm = pl.BlockSpec(memory_space=pl.ANY)
    dma = pltpu.SemaphoreType.DMA
    part = pltpu.VMEM((lines, rows, width), BF16)
    return pl.pallas_call(
        functools.partial(mlp_kernel, lines),
        out_shape=jax.ShapeDtypeStruct((rows, width), BF16),
        in_specs=[vmem, hbm, hbm, vmem],
        out_specs=vmem,
        scratch_shapes=[
            pltpu.VMEM((devices * rows, width), BF16),
            pltpu.VMEM(w_gate_up.shape, BF16),
            pltpu.VMEM(w_down.shape, BF16),
            pltpu.VMEM((2 * rows, units), BF16),
            pltpu.VMEM((2 * rows, width), F32),
            pltpu.VMEM((lines, rows, width), F32),
            part, part, part, part,
            dma((3,)),
            dma((3, devices)),
            dma((devices,)),
            dma((lines,)),
            dma((lines,)),
            dma((lines,)),
            dma((lines,)),
        ],
        compiler_params=pltpu.CompilerParams(
            collective_id=1, has_side_effects=True, vmem_limit_bytes=60 * 2**20
        ),
    )(mid_state, w_gate_up, w_down, gain)


def tree_info(leaf_segment, leaf_node, node_parent, node_length):
    groups, tok_rows = leaf_segment.shape
    leaf_count = leaf_node.shape[1]
    middles = node_parent.shape[0]
    all_nodes = node_length.shape[0]
    tenant_count = all_nodes - middles
    leaf_ids = jnp.arange(leaf_count, dtype=jnp.int32)
    onehot = (leaf_segment[:, :, None] == leaf_ids[None, None, :]).astype(jnp.int32)
    middle = jnp.sum(onehot * leaf_node[:, None, :], axis=-1)
    counts = jnp.sum(onehot, axis=1)
    starts = jnp.cumsum(counts, axis=1) - counts
    first_at = jnp.sum(onehot * starts[:, None, :], axis=-1)
    middle_ids = jnp.arange(middles, dtype=jnp.int32) + tenant_count
    root_node = jnp.sum(jnp.where(middle[..., None] == middle_ids, node_parent, 0), axis=-1)
    node_ids = jnp.arange(all_nodes, dtype=jnp.int32)
    len_middle = jnp.sum(jnp.where(middle[..., None] == node_ids, node_length, 0), axis=-1)
    len_root = jnp.sum(jnp.where(root_node[..., None] == node_ids, node_length, 0), axis=-1)
    offsets = jnp.arange(tok_rows, dtype=jnp.int32)[None, :] - first_at
    position = len_root + len_middle + offsets
    return (middle, root_node, position)


def rotate(values_in, position):
    half_size = values_in.shape[-1] // 2
    frequency = THETA ** (-2.0 * jnp.arange(half_size, dtype=jnp.float32) / values_in.shape[-1])
    angles = position.astype(jnp.float32)[:, None] * frequency[None, :]
    cosine = jnp.cos(angles)[:, None, :]
    sine_part = jnp.sin(angles)[:, None, :]
    lower = values_in[..., :half_size]
    upper = values_in[..., half_size:]
    return jnp.concatenate(
        [lower * cosine - upper * sine_part, upper * cosine + lower * sine_part], axis=-1
    )


def rms_norm(values_in, gain):
    return (
        values_in * lax.rsqrt(jnp.mean(values_in * values_in, axis=-1, keepdims=True) + EPS) * gain
    )


def lookup_length(nodes, node_length):
    node_ids = jnp.arange(node_length.shape[0], dtype=jnp.int32)
    return jnp.sum(jnp.where(nodes[:, None] == node_ids[None, :], node_length[None, :], 0), axis=-1)


def masked_partial(scores, visible, values_in):
    masked = jnp.where(visible, scores, NEG)
    peak = jnp.max(masked, axis=-1)
    weights = jnp.where(visible, jnp.exp(masked - peak[..., None]), 0.0)
    totals = jnp.sum(weights, axis=-1)
    summed = jnp.einsum(
        "rhk,khe->rhe", weights.astype(jnp.bfloat16), values_in, preferred_element_type=jnp.float32
    )
    return (peak, totals, summed)


def combine(left, right):
    peak = jnp.maximum(left[0], right[0])
    scale_left = jnp.exp(left[0] - peak)
    scale_right = jnp.exp(right[0] - peak)
    totals = left[1] * scale_left + right[1] * scale_right
    summed = left[2] * scale_left[..., None] + right[2] * scale_right[..., None]
    return (peak, totals, summed)


def cache_partial(queries, middle, root_node, keys_in, values_in, nodes, lengths):
    slots, node_rows, columns = keys_in.shape
    head_count, size = (queries.shape[1], queries.shape[2])
    flat_keys = keys_in.reshape(slots * node_rows, head_count, size)
    flat_values = values_in.reshape(slots * node_rows, head_count, size)
    node_flat = jnp.broadcast_to(nodes[:, None], (slots, node_rows)).reshape(-1)
    length_flat = jnp.broadcast_to(lengths[:, None], (slots, node_rows)).reshape(-1)
    row_flat = jnp.broadcast_to(
        jnp.arange(node_rows, dtype=jnp.int32)[None, :], (slots, node_rows)
    ).reshape(-1)
    visible = (
        (node_flat[None, :] == middle[:, None]) | (node_flat[None, :] == root_node[:, None])
    ) & (row_flat < length_flat)[None, :]
    scores = jnp.einsum(
        "rhe,khe->rhk", queries, flat_keys, preferred_element_type=jnp.float32
    ) * size ** (-0.5)
    return masked_partial(scores, visible[:, None, :], flat_values)


def on_device(
    states_in,
    w_qkv,
    qk_gain,
    w_out,
    post_gain,
    w_gate_up,
    w_down,
    cache_keys,
    cache_values,
    slot_node,
    node_length,
    node_parent,
    leaf_segment,
    leaf_node,
):
    blk_index = lax.axis_index("blk")
    head_index = lax.axis_index("head")
    head_devices = lax.axis_size("head")
    tok_rows = states_in.shape[0]
    heads_here = w_qkv.shape[2] // HD
    columns = w_qkv.shape[2] * head_devices
    qkv_raw = jnp.einsum("td,cdw->ctw", states_in, w_qkv, preferred_element_type=jnp.float32)
    query_squares, key_squares = lax.psum(
        (jnp.sum(qkv_raw[0] * qkv_raw[0], axis=1), jnp.sum(qkv_raw[1] * qkv_raw[1], axis=1)), "head"
    )
    middle_all, root_all, position_all = tree_info(
        leaf_segment, leaf_node, node_parent, node_length
    )
    position = lax.dynamic_index_in_dim(position_all, blk_index, 0, keepdims=False)
    middle_own = lax.dynamic_index_in_dim(middle_all, blk_index, 0, keepdims=False)
    root_own = lax.dynamic_index_in_dim(root_all, blk_index, 0, keepdims=False)
    segment_own = lax.dynamic_index_in_dim(leaf_segment, blk_index, 0, keepdims=False)

    def normed(raw_part, squares, gain):
        scaled = raw_part * lax.rsqrt(squares / columns + EPS)[:, None] * gain
        return rotate(scaled.reshape(tok_rows, heads_here, HD), position).astype(jnp.bfloat16)

    queries = normed(qkv_raw[0], query_squares, qk_gain[0])
    keys_new = normed(qkv_raw[1], key_squares, qk_gain[1])
    values_cast = qkv_raw[2].astype(jnp.bfloat16).reshape(tok_rows, heads_here, HD)
    order = jnp.arange(tok_rows, dtype=jnp.int32)
    see_leaf = (segment_own[:, None] == segment_own[None, :]) & (order[None, :] <= order[:, None])
    leaf_scores = jnp.einsum(
        "rhe,khe->rhk", queries, keys_new, preferred_element_type=jnp.float32
    ) * HD ** (-0.5)
    local_state = masked_partial(leaf_scores, see_leaf[:, None, :], values_cast)
    keys_piece = lax.all_gather(cache_keys, "blk", axis=0, tiled=True)
    values_piece = lax.all_gather(cache_values, "blk", axis=0, tiled=True)
    lengths = lookup_length(slot_node, node_length)
    needed = jnp.any(
        (slot_node[:, None] == middle_own[None, :]) | (slot_node[:, None] == root_own[None, :])
    )

    def attend(carry):
        return combine(
            carry,
            cache_partial(
                queries, middle_own, root_own, keys_piece, values_piece, slot_node, lengths
            ),
        )

    def keep(carry):
        return carry

    state = lax.cond(needed, attend, keep, local_state)
    attended = (
        (state[2] / state[1][..., None]).astype(jnp.bfloat16).reshape(tok_rows, heads_here * HD)
    )
    attn_part = jnp.dot(attended, w_out, preferred_element_type=jnp.float32)
    own_rows = tok_rows // head_devices
    attn_whole = lax.psum(attn_part.astype(jnp.bfloat16), "head").astype(jnp.float32)
    attn_proj = lax.dynamic_slice_in_dim(attn_whole, head_index * own_rows, own_rows, 0)
    state_rows = lax.dynamic_slice_in_dim(states_in, head_index * own_rows, own_rows, 0)
    mid_state = (state_rows.astype(jnp.float32) + rms_norm(attn_proj, post_gain[0])).astype(
        jnp.bfloat16
    )
    return mlp(mid_state, w_gate_up, w_down, post_gain[1:2], lax.axis_size("blk"))


def solution(mesh):
    placed = (
        P("blk", None),
        P(None, None, "head"),
        P(None, "head"),
        P("head", None),
        P(),
        P(None, None, "blk"),
        P("blk", None),
        P("blk", None, "head"),
        P("blk", None, "head"),
        P(),
        P(),
        P(),
        P(),
        P(),
    )
    return jax.shard_map(
        on_device, mesh=mesh, in_specs=placed, out_specs=P(("blk", "head"), None), check_vma=False
    )
```

```python
import functools

import jax
import jax.numpy as jnp
from jax import lax
from jax.experimental import pallas as pl
from jax.experimental.pallas import tpu as pltpu
from jax.sharding import PartitionSpec as P

HD = 128
EPS = 1e-06
THETA = 500000.0
NEG = -1e30
MESH = pl.DeviceIdType.MESH
BF16 = jnp.bfloat16
F32 = jnp.float32


def by_distance(at, count, step):
    back = count - 1 - at
    near = jnp.minimum(at, back)
    both = jnp.where(step % 2 == 1, at - (step + 1) // 2, at + step // 2)
    return jnp.where(step <= 2 * near, both, jnp.where(at < back, step, count - 1 - step))


def remote(src, dst, send_sem, recv_sem, **where):
    return pltpu.make_async_remote_copy(
        src_ref=src,
        dst_ref=dst,
        send_sem=send_sem,
        recv_sem=recv_sem,
        device_id=where,
        device_id_type=MESH,
    )


def meet(peers):
    barrier = pltpu.get_barrier_semaphore()
    for peer in peers:
        pl.semaphore_signal(barrier, inc=1, device_id=peer, device_id_type=MESH)
    pl.semaphore_wait(barrier, len(peers))


def mlp_kernel(
    lines,
    mid_ref, wgu_hbm, wd_hbm, gain_ref, out_ref,
    gathered, wgu, wd, hidden, whole, own_part, send_x, recv_x, send_z, recv_z,
    w_sem, g_send, g_recv, x_send, x_recv, z_send, z_recv,
):
    rows, width = mid_ref.shape
    units = wd.shape[0]
    me = lax.axis_index("blk")
    z, x = me // 2, me % 2
    other = z * 2 + 1 - x

    loads = [
        pltpu.make_async_copy(wgu_hbm.at[0], wgu.at[0], w_sem.at[0]),
        pltpu.make_async_copy(wgu_hbm.at[1], wgu.at[1], w_sem.at[1]),
        pltpu.make_async_copy(wd_hbm, wd, w_sem.at[2]),
    ]
    for load in loads:
        load.start()
    meet([{"blk": other}] + [{"blk": (z + j) % lines * 2 + x} for j in range(1, lines)])

    def block(index):
        return gathered.at[pl.ds(pl.multiple_of(index * rows, rows), rows)]

    def pass_on(index, way, target):
        return remote(block(index), block(index), g_send.at[way, index], g_recv.at[index], blk=target)

    def spread(origin, wait):
        index = origin * 2 + x
        if wait:
            pass_on(index, 0, other).wait_recv()
        pass_on(index, 0, other).start()

        @pl.when((origin <= z) & (z < lines - 1))
        def _():
            pass_on(index, 1, me + 2).start()

        @pl.when((origin >= z) & (z > 0))
        def _():
            pass_on(index, 2, me - 2).start()

    gathered[pl.ds(pl.multiple_of(me * rows, rows), rows), :] = mid_ref[...]
    spread(z, False)

    def to_x(origin):
        return remote(send_x.at[origin], recv_x.at[origin], x_send.at[origin], x_recv.at[origin], blk=other)

    def to_z(origin):
        return remote(send_z.at[origin], recv_z.at[z], z_send.at[origin], z_recv.at[z], blk=origin * 2 + x)

    def reduce_x(origin):
        to_x(origin).wait_recv()
        summed = own_part[origin] + recv_x[origin].astype(F32)
        own_part[origin] = summed
        send_z[origin] = summed.astype(BF16)

        @pl.when(origin != z)
        def _():
            to_z(origin).start()

    tile = min(256, units)
    wide = min(512, width)
    for step in range(lines):
        origin = by_distance(z, lines, step)
        if step + 1 < lines:
            spread(by_distance(z, lines, step + 1), True)
        pass_on(origin * 2 + 1 - x, 0, other).wait_recv()
        if step == 0:
            loads[0].wait()
            loads[1].wait()
        chunk = pl.ds(pl.multiple_of(origin * 2 * rows, 2 * rows), 2 * rows)

        @pl.loop(0, units // tile)
        def _(t):
            at = pl.ds(pl.multiple_of(t * tile, tile), tile)
            state = gathered[chunk, :]
            gate = jnp.dot(state, wgu[0, :, at], preferred_element_type=F32)
            up = jnp.dot(state, wgu[1, :, at], preferred_element_type=F32)
            hidden[:, at] = (gate / (1.0 + jnp.exp(-gate)) * up).astype(BF16)

        if step == 0:
            loads[2].wait()

        @pl.loop(0, width // wide)
        def _(t):
            at = pl.ds(pl.multiple_of(t * wide, wide), wide)
            whole[:, at] = jnp.dot(hidden[...], wd[:, at], preferred_element_type=F32)

        own_part[origin] = whole[pl.ds(pl.multiple_of(x * rows, rows), rows), :]
        send_x[origin] = whole[pl.ds(pl.multiple_of((1 - x) * rows, rows), rows), :].astype(BF16)
        to_x(origin).start()
        if step > 0:
            reduce_x(by_distance(z, lines, step - 1))
    reduce_x(by_distance(z, lines, lines - 1))

    total = own_part[z]
    for j in range(1, lines):
        source = (z + j) % lines
        remote(send_z.at[0], recv_z.at[source], z_send.at[0], z_recv.at[source], blk=other).wait_recv()
        total = total + recv_z[source].astype(F32)
    scale = lax.rsqrt(jnp.mean(total * total, axis=-1, keepdims=True) + EPS)
    out_ref[...] = (mid_ref[...].astype(F32) + total * scale * gain_ref[...]).astype(BF16)

    for origin in range(lines):
        index = origin * 2 + x
        to_x(origin).wait_send()
        pass_on(index, 0, other).wait_send()

        @pl.when((origin <= z) & (z < lines - 1))
        def _():
            pass_on(index, 1, me + 2).wait_send()

        @pl.when((origin >= z) & (z > 0))
        def _():
            pass_on(index, 2, me - 2).wait_send()

        @pl.when(origin != z)
        def _():
            to_z(origin).wait_send()


def mlp(mid_state, w_gate_up, w_down, gain, devices):
    rows, width = mid_state.shape
    units = w_down.shape[0]
    lines = devices // 2
    vmem = pl.BlockSpec(memory_space=pltpu.VMEM)
    hbm = pl.BlockSpec(memory_space=pl.ANY)
    dma = pltpu.SemaphoreType.DMA
    part = pltpu.VMEM((lines, rows, width), BF16)
    return pl.pallas_call(
        functools.partial(mlp_kernel, lines),
        out_shape=jax.ShapeDtypeStruct((rows, width), BF16),
        in_specs=[vmem, hbm, hbm, vmem],
        out_specs=vmem,
        scratch_shapes=[
            pltpu.VMEM((devices * rows, width), BF16),
            pltpu.VMEM(w_gate_up.shape, BF16),
            pltpu.VMEM(w_down.shape, BF16),
            pltpu.VMEM((2 * rows, units), BF16),
            pltpu.VMEM((2 * rows, width), F32),
            pltpu.VMEM((lines, rows, width), F32),
            part, part, part, part,
            dma((3,)),
            dma((3, devices)),
            dma((devices,)),
            dma((lines,)),
            dma((lines,)),
            dma((lines,)),
            dma((lines,)),
        ],
        compiler_params=pltpu.CompilerParams(
            collective_id=1, has_side_effects=True, vmem_limit_bytes=60 * 2**20
        ),
    )(mid_state, w_gate_up, w_down, gain)


def attention_kernel(
    spread_count,
    states_ref, wqkv_hbm, gain_ref, cos_ref, sin_ref, first_ref, limit_ref, keys_hbm, values_hbm,
    wout_hbm, post_ref, out_ref,
    wqkv, wout, raw, query, key, value, squares, query_in, keys_in, values_in,
    peak, norm, acc, leaf_peak, leaf_norm, leaf_acc, part_out, part_in, stat_out, stat_in,
    attended, proj, proj_low, pair_in, pair_out, line_in,
    w_sem, s_send, s_recv, q_send, q_recv, own_sem, k_send, k_recv, v_send, v_recv,
    p_send, p_recv, t_send, t_recv, c_send, c_recv, y_send, y_recv,
):
    rows, width = states_ref.shape
    heads = query.shape[0]
    node_rows = keys_hbm.shape[1]
    slots = keys_in.shape[0]
    me = lax.axis_index("blk")
    head = lax.axis_index("head")
    mine, rest = me // spread_count, me % spread_count
    scale = HD ** (-0.5)

    loads = [pltpu.make_async_copy(wqkv_hbm.at[c], wqkv.at[c], w_sem.at[c]) for c in range(3)]
    loads.append(pltpu.make_async_copy(wout_hbm, wout, w_sem.at[3]))
    for load in loads:
        load.start()

    def holder(index):
        return index * spread_count + rest

    peers = [{"head": (head + j) % 4} for j in range(1, 4)]
    peers += [{"blk": holder((mine + j) % heads)} for j in range(1, heads)]
    peers += [{"blk": mine * spread_count + (rest + j) % spread_count} for j in range(1, spread_count)]
    meet(peers)

    def column(index):
        return pl.ds(pl.multiple_of(index * HD, HD), HD)

    def cache_out(target):
        return (
            remote(keys_hbm.at[0, :, column(target)], keys_in.at[me], k_send.at[0, target], k_recv.at[me], blk=holder(target)),
            remote(values_hbm.at[0, :, column(target)], values_in.at[me], v_send.at[0, target], v_recv.at[me], blk=holder(target)),
        )

    def cache_wait(slot):
        far = holder((mine + 1) % heads)
        remote(keys_in.at[slot], keys_in.at[slot], k_send.at[0, 0], k_recv.at[slot], blk=far).wait_recv()
        remote(values_in.at[slot], values_in.at[slot], v_send.at[0, 0], v_recv.at[slot], blk=far).wait_recv()

    def cache_on(source, j):
        slot = holder(source)
        target = mine * spread_count + (rest + j) % spread_count
        return (
            remote(keys_in.at[slot], keys_in.at[slot], k_send.at[j, source], k_recv.at[slot], blk=target),
            remote(values_in.at[slot], values_in.at[slot], v_send.at[j, source], v_recv.at[slot], blk=target),
        )

    for j in range(1, heads):
        for copy in cache_out((mine + j) % heads):
            copy.start()
    own_copies = [
        pltpu.make_async_copy(keys_hbm.at[0, :, column(mine)], keys_in.at[me], own_sem.at[0]),
        pltpu.make_async_copy(values_hbm.at[0, :, column(mine)], values_in.at[me], own_sem.at[1]),
    ]
    for copy in own_copies:
        copy.start()

    def pass_on(step):
        source = by_distance(mine, heads, step)
        if step == 0:
            for copy in own_copies:
                copy.wait()
        else:
            cache_wait(holder(source))
        for j in range(1, spread_count):
            for copy in cache_on(source, j):
                copy.start()

    tile = 2 * HD
    here = heads * HD

    def product(c):
        loads[c].wait()

        @pl.loop(0, here // tile)
        def _(t):
            at = pl.ds(pl.multiple_of(t * tile, tile), tile)
            raw[c, :, at] = jnp.dot(states_ref[...], wqkv[c, :, at], preferred_element_type=F32)

    lane = lax.broadcasted_iota(jnp.int32, (rows, HD), 1)
    product(0)
    pass_on(0)
    product(1)
    query_sum = jnp.sum(raw[0] * raw[0], axis=-1, keepdims=True)
    key_sum = jnp.sum(raw[1] * raw[1], axis=-1, keepdims=True)
    packed = jnp.where(lane == 0, query_sum, jnp.where(lane == 1, key_sum, 0.0))
    squares[head] = jnp.transpose(packed)[0:8]

    def squares_to(target):
        return remote(squares.at[head], squares.at[head], s_send.at[target], s_recv.at[head], head=target)

    for j in range(1, 4):
        squares_to((head + j) % 4).start()
    product(2)
    value[...] = raw[2].astype(BF16)
    pass_on(1)
    total = squares[head]
    for j in range(1, 4):
        source = (head + j) % 4
        remote(squares.at[source], squares.at[source], s_send.at[source], s_recv.at[source], head=source).wait_recv()
        total = total + squares[source]
    spread = jnp.transpose(jnp.concatenate([total] * (HD // 8), axis=0))
    scales = lax.rsqrt(spread / width + EPS)
    query_scale, key_scale = scales[:, 0:1], scales[:, 1:2]

    def turned(c, h, by):
        at = slice(h * HD, (h + 1) * HD)
        normed = raw[c, :, at] * by * gain_ref[c : c + 1, at]
        swapped = pltpu.roll(normed, HD // 2, 1)
        return (normed * cos_ref[...] + swapped * sin_ref[...]).astype(BF16)

    for h in range(heads):
        query[h] = turned(0, h, query_scale)

    def query_to(target):
        return remote(query.at[target], query_in.at[mine], q_send.at[target], q_recv.at[mine], blk=holder(target))

    for j in range(1, heads):
        query_to((mine + j) % heads).start()
    query_in[mine] = query[mine]
    for h in range(heads):
        key[h] = turned(1, h, key_scale)
    pass_on(2)

    row_at = lax.broadcasted_iota(jnp.int32, (rows, rows), 0)
    key_at = lax.broadcasted_iota(jnp.int32, (rows, rows), 1)
    see_leaf = (key_at >= first_ref[...]) & (key_at <= row_at)
    over = (((1,), (1,)), ((), ()))
    for h in range(heads):
        scores = lax.dot_general(query[h], key[h], over, preferred_element_type=F32) * scale
        scores = jnp.where(see_leaf, scores, NEG)
        top = jnp.max(scores, axis=-1, keepdims=True)
        weights = jnp.exp(scores - top)
        leaf_peak[h] = jnp.broadcast_to(top, (rows, HD))
        leaf_norm[h] = jnp.broadcast_to(jnp.sum(weights, axis=-1, keepdims=True), (rows, HD))
        leaf_acc[h] = jnp.dot(weights.astype(BF16), value[:, h * HD : (h + 1) * HD], preferred_element_type=F32)
        if h == 1:
            for step in range(3, heads):
                pass_on(step)

    for j in range(1, heads):
        source = (mine + j) % heads
        remote(query.at[0], query_in.at[source], q_send.at[0], q_recv.at[source], blk=holder(source)).wait_recv()
    peak[...] = jnp.full(peak.shape, NEG, F32)
    norm[...] = jnp.zeros(norm.shape, F32)
    acc[...] = jnp.zeros(acc.shape, F32)
    key_row = lax.broadcasted_iota(jnp.int32, (rows, node_rows), 1)
    slot_lane = lax.broadcasted_iota(jnp.int32, (rows, slots), 1)

    def look_at(slot):
        @pl.loop(0, heads)
        def _(g):
            limit = jnp.max(jnp.where(slot_lane == slot, limit_ref[g], 0), axis=-1, keepdims=True)
            scores = lax.dot_general(query_in[g], keys_in[slot], over, preferred_element_type=F32) * scale
            scores = jnp.where(key_row < limit, scores, NEG)
            before = peak[g]
            top = jnp.maximum(before, jnp.max(scores, axis=-1, keepdims=True))
            weights = jnp.exp(scores - top[:, 0:1])
            shrink = jnp.exp(before - top)
            peak[g] = top
            norm[g] = norm[g] * shrink + jnp.sum(weights, axis=-1, keepdims=True)
            acc[g] = acc[g] * shrink + jnp.dot(
                weights.astype(BF16), values_in[slot], preferred_element_type=F32
            )

    for step in range(heads):
        look_at(holder(by_distance(mine, heads, step)))
    for step in range(heads):
        for j in range(1, spread_count):
            slot = by_distance(mine, heads, step) * spread_count + (rest + j) % spread_count
            cache_wait(slot)
            look_at(slot)

    def part_to(target):
        return (
            remote(part_out.at[target], part_in.at[mine], p_send.at[target], p_recv.at[mine], blk=holder(target)),
            remote(stat_out.at[target], stat_in.at[mine], t_send.at[target], t_recv.at[mine], blk=holder(target)),
        )

    for j in list(range(1, heads)) + [0]:
        g = (mine + j) % heads
        part_out[g] = (acc[g] / norm[g]).astype(BF16)
        stats = jnp.where(lane == 0, peak[g], jnp.where(lane == 1, norm[g], 0.0))
        stat_out[g] = jnp.transpose(stats)[0:8]
        if j > 0:
            for copy in part_to(g):
                copy.start()
        else:
            part_in[g] = part_out[g]
            stat_in[g] = stat_out[g]
    for j in range(1, heads):
        source = (mine + j) % heads
        remote(part_out.at[0], part_in.at[source], p_send.at[0], p_recv.at[source], blk=holder(source)).wait_recv()
        remote(stat_out.at[0], stat_in.at[source], t_send.at[0], t_recv.at[source], blk=holder(source)).wait_recv()
    for h in range(heads):
        stats = jnp.transpose(jnp.concatenate([stat_in[h]] * (HD // 8), axis=0))
        other_peak, other_norm = stats[:, 0:1], stats[:, 1:2]
        top = jnp.maximum(leaf_peak[h], other_peak)
        own_scale = jnp.exp(leaf_peak[h] - top)
        other_scale = jnp.exp(other_peak - top) * other_norm
        summed = leaf_acc[h] * own_scale + part_in[h].astype(F32) * other_scale
        attended[:, h * HD : (h + 1) * HD] = (
            summed / (leaf_norm[h] * own_scale + other_scale)
        ).astype(BF16)

    loads[3].wait()
    wide = min(512, width)

    @pl.loop(0, width // wide)
    def _(t):
        at = pl.ds(pl.multiple_of(t * wide, wide), wide)
        tiled = jnp.dot(attended[...], wout[:, at], preferred_element_type=F32)
        proj[:, at] = tiled
        proj_low[:, at] = tiled.astype(BF16)

    y, core = head // 2, head % 2
    own_rows = out_ref.shape[0]
    sibling, across = y * 2 + 1 - core, (1 - y) * 2 + core

    def rows_of(index):
        return pl.ds(pl.multiple_of(index * own_rows, own_rows), own_rows)

    def to_pair(half):
        return remote(proj_low.at[rows_of(half * 2 + 1 - core)], pair_in.at[half], c_send.at[half], c_recv.at[half], head=sibling)

    to_pair(1 - y).start()
    to_pair(y).start()
    to_pair(1 - y).wait_recv()
    pair_out[...] = (proj[rows_of(across), :] + pair_in[1 - y].astype(F32)).astype(BF16)
    over_y = remote(pair_out, line_in, y_send.at[0], y_recv.at[0], head=across)
    over_y.start()
    to_pair(y).wait_recv()
    total = proj[rows_of(head), :] + pair_in[y].astype(F32)
    over_y.wait_recv()
    total = total + line_in[...].astype(F32)
    shrink = lax.rsqrt(jnp.mean(total * total, axis=-1, keepdims=True) + EPS)
    own = states_ref[rows_of(head), :].astype(F32)
    out_ref[...] = (own + total * shrink * post_ref[...]).astype(BF16)

    over_y.wait_send()
    for half in range(2):
        to_pair(half).wait_send()
    for j in range(1, 4):
        squares_to((head + j) % 4).wait_send()
    for j in range(1, heads):
        target = (mine + j) % heads
        query_to(target).wait_send()
        for copy in cache_out(target) + part_to(target):
            copy.wait_send()
    for source in range(heads):
        for j in range(1, spread_count):
            for copy in cache_on(source, j):
                copy.wait_send()


def attention(states_in, w_qkv, qk_gain, cosine, sine, first, limits, cache_keys, cache_values, w_out, gain, slots):
    rows, width = states_in.shape
    here = w_qkv.shape[2]
    heads = here // HD
    node_rows = cache_keys.shape[1]
    own_rows = rows // 4
    vmem = pl.BlockSpec(memory_space=pltpu.VMEM)
    hbm = pl.BlockSpec(memory_space=pl.ANY)
    dma = pltpu.SemaphoreType.DMA
    spread_count = slots // heads

    def per_head(kind):
        return pltpu.VMEM((heads, rows, HD), kind)

    return pl.pallas_call(
        functools.partial(attention_kernel, spread_count),
        out_shape=jax.ShapeDtypeStruct((own_rows, width), BF16),
        in_specs=[vmem, hbm, vmem, vmem, vmem, vmem, vmem, hbm, hbm, hbm, vmem],
        out_specs=vmem,
        scratch_shapes=[
            pltpu.VMEM(w_qkv.shape, BF16),
            pltpu.VMEM(w_out.shape, BF16),
            pltpu.VMEM((3, rows, here), F32),
            per_head(BF16),
            per_head(BF16),
            pltpu.VMEM((rows, here), BF16),
            pltpu.VMEM((4, 8, rows), F32),
            per_head(BF16),
            pltpu.VMEM((slots, node_rows, HD), BF16),
            pltpu.VMEM((slots, node_rows, HD), BF16),
            per_head(F32), per_head(F32), per_head(F32),
            per_head(F32), per_head(F32), per_head(F32),
            per_head(BF16), per_head(BF16),
            pltpu.VMEM((heads, 8, rows), F32),
            pltpu.VMEM((heads, 8, rows), F32),
            pltpu.VMEM((rows, here), BF16),
            pltpu.VMEM((rows, width), F32),
            pltpu.VMEM((rows, width), BF16),
            pltpu.VMEM((2, own_rows, width), BF16),
            pltpu.VMEM((own_rows, width), BF16),
            pltpu.VMEM((own_rows, width), BF16),
            dma((4,)),
            dma((4,)), dma((4,)),
            dma((heads,)), dma((heads,)),
            dma((2,)),
            dma((spread_count, heads)), dma((slots,)),
            dma((spread_count, heads)), dma((slots,)),
            dma((heads,)), dma((heads,)),
            dma((heads,)), dma((heads,)),
            dma((2,)), dma((2,)),
            dma((1,)), dma((1,)),
        ],
        compiler_params=pltpu.CompilerParams(
            collective_id=2, has_side_effects=True, vmem_limit_bytes=60 * 2**20
        ),
    )(states_in, w_qkv, qk_gain, cosine, sine, first, limits, cache_keys, cache_values, w_out, gain)


def on_device(
    states_in,
    w_qkv,
    qk_gain,
    w_out,
    post_gain,
    w_gate_up,
    w_down,
    cache_keys,
    cache_values,
    slot_node,
    node_length,
    node_parent,
    leaf_segment,
    leaf_node,
):
    blk_index = lax.axis_index("blk")
    devices = lax.axis_size("blk")
    heads = w_qkv.shape[2] // HD
    spread_count = devices // heads
    mine, rest = blk_index // spread_count, blk_index % spread_count
    tok_rows = leaf_segment.shape[1]
    leaves = leaf_node.shape[1]
    middles = node_parent.shape[0]
    nodes = node_length.shape[0]
    segments = lax.dynamic_index_in_dim(leaf_segment.reshape(heads, spread_count, tok_rows), rest, 1, keepdims=False)
    hangs = lax.dynamic_index_in_dim(leaf_node.reshape(heads, spread_count, leaves), rest, 1, keepdims=False)
    node_ids = jnp.arange(nodes, dtype=jnp.int32)
    middle_ids = jnp.arange(middles, dtype=jnp.int32) + (nodes - middles)
    roots = jnp.sum(jnp.where(hangs[..., None] == middle_ids, node_parent, 0), axis=-1)
    lengths = jnp.sum(jnp.where(slot_node[:, None] == node_ids[None, :], node_length[None, :], 0), axis=-1)
    seen = (slot_node == hangs[..., None]) | (slot_node == roots[..., None])
    leaf_limits = jnp.where(seen, lengths, 0)
    leaf_ids = jnp.arange(leaves, dtype=jnp.int32)
    onehot = segments[:, :, None] == leaf_ids
    limits = jnp.sum(jnp.where(onehot[..., None], leaf_limits[:, None], 0), axis=2)
    segment = lax.dynamic_index_in_dim(segments, mine, 0, keepdims=False)
    first = jnp.sum((segment[None, :] < segment[:, None]).astype(jnp.int32), axis=-1)
    before = jnp.sum(lax.dynamic_index_in_dim(limits, mine, 0, keepdims=False), axis=-1)
    position = before + jnp.arange(tok_rows, dtype=jnp.int32) - first
    half = HD // 2
    frequency = THETA ** (-2.0 * jnp.arange(half, dtype=F32) / HD)
    angles = position.astype(F32)[:, None] * frequency[None, :]
    cosine, sine = jnp.cos(angles), jnp.sin(angles)
    mid_state = attention(
        states_in,
        w_qkv,
        qk_gain,
        jnp.concatenate([cosine, cosine], axis=-1),
        jnp.concatenate([-sine, sine], axis=-1),
        first[:, None],
        limits,
        cache_keys,
        cache_values,
        w_out,
        post_gain[0:1],
        devices,
    )
    return mlp(mid_state, w_gate_up, w_down, post_gain[1:2], devices)


def solution(mesh):
    placed = (
        P("blk", None),
        P(None, None, "head"),
        P(None, "head"),
        P("head", None),
        P(),
        P(None, None, "blk"),
        P("blk", None),
        P("blk", None, "head"),
        P("blk", None, "head"),
        P(),
        P(),
        P(),
        P(),
        P(),
    )
    return jax.shard_map(
        on_device, mesh=mesh, in_specs=placed, out_specs=P(("blk", "head"), None), check_vma=False
    )
```

```python
import functools

import jax
import jax.numpy as jnp
from jax import lax
from jax.experimental import pallas as pl
from jax.experimental.pallas import tpu as pltpu
from jax.sharding import PartitionSpec as P

HD = 128
EPS = 1e-06
THETA = 500000.0
NEG = -1e30
MESH = pl.DeviceIdType.MESH
BF16 = jnp.bfloat16
F32 = jnp.float32


def by_distance(at, count, step):
    back = count - 1 - at
    near = jnp.minimum(at, back)
    both = jnp.where(step % 2 == 1, at - (step + 1) // 2, at + step // 2)
    return jnp.where(step <= 2 * near, both, jnp.where(at < back, step, count - 1 - step))


def remote(src, dst, send_sem, recv_sem, **where):
    return pltpu.make_async_remote_copy(
        src_ref=src,
        dst_ref=dst,
        send_sem=send_sem,
        recv_sem=recv_sem,
        device_id=where,
        device_id_type=MESH,
    )


def meet(peers):
    barrier = pltpu.get_barrier_semaphore()
    for peer in peers:
        pl.semaphore_signal(barrier, inc=1, device_id=peer, device_id_type=MESH)
    pl.semaphore_wait(barrier, len(peers))


def mlp_part(
    lines, loads,
    mid_ref, gain_ref, out_ref,
    gathered, wgu, wd, hidden, whole, own_part, own_sum, send_x, recv_x, recv_z,
    g_send, g_recv, x_send, x_recv, z_send, z_recv,
):
    rows, width = mid_ref.shape
    units = wd.shape[0]
    me = lax.axis_index("blk")
    z, x = me // 2, me % 2
    other = z * 2 + 1 - x

    def block(index):
        return gathered.at[pl.ds(pl.multiple_of(index * rows, rows), rows)]

    def pass_on(index, way, target):
        return remote(block(index), block(index), g_send.at[way, index], g_recv.at[index], blk=target)

    def spread(origin, wait):
        index = origin * 2 + x
        if wait:
            pass_on(index, 0, other).wait_recv()
        pass_on(index, 0, other).start()

        @pl.when((origin <= z) & (z < lines - 1))
        def _():
            pass_on(index, 1, me + 2).start()

        @pl.when((origin >= z) & (z > 0))
        def _():
            pass_on(index, 2, me - 2).start()

    gathered[pl.ds(pl.multiple_of(me * rows, rows), rows), :] = mid_ref[...]
    spread(z, False)

    def to_x(origin):
        return remote(send_x.at[origin], recv_x.at[origin], x_send.at[origin], x_recv.at[origin], blk=other)

    def to_z(origin):
        return remote(send_x.at[origin], recv_z.at[z], z_send.at[origin], z_recv.at[z], blk=origin * 2 + x)

    def reduce_x(step):
        origin = by_distance(z, lines, step)
        to_x(origin).wait_recv()
        summed = own_part[step % 2] + recv_x[origin].astype(F32)
        to_x(origin).wait_send()
        if step == 0:
            own_sum[...] = summed
        else:
            send_x[origin] = summed.astype(BF16)
            to_z(origin).start()

    tile = min(256, units)
    wide = min(512, width)
    for step in range(lines):
        origin = by_distance(z, lines, step)
        if step + 1 < lines:
            spread(by_distance(z, lines, step + 1), True)
        pass_on(origin * 2 + 1 - x, 0, other).wait_recv()
        if step == 0:
            loads[0].wait()
            loads[1].wait()
        chunk = pl.ds(pl.multiple_of(origin * 2 * rows, 2 * rows), 2 * rows)

        @pl.loop(0, units // tile)
        def _(t):
            at = pl.ds(pl.multiple_of(t * tile, tile), tile)
            state = gathered[chunk, :]
            gate = jnp.dot(state, wgu[0, :, at], preferred_element_type=F32)
            up = jnp.dot(state, wgu[1, :, at], preferred_element_type=F32)
            hidden[:, at] = (gate / (1.0 + jnp.exp(-gate)) * up).astype(BF16)

        if step == 0:
            loads[2].wait()

        @pl.loop(0, width // wide)
        def _(t):
            at = pl.ds(pl.multiple_of(t * wide, wide), wide)
            whole[:, at] = jnp.dot(hidden[...], wd[:, at], preferred_element_type=F32)

        own_part[step % 2] = whole[pl.ds(pl.multiple_of(x * rows, rows), rows), :]
        send_x[origin] = whole[pl.ds(pl.multiple_of((1 - x) * rows, rows), rows), :].astype(BF16)
        to_x(origin).start()
        if step > 0:
            reduce_x(step - 1)
    reduce_x(lines - 1)

    total = own_sum[...]
    for j in range(1, lines):
        source = (z + j) % lines
        remote(send_x.at[0], recv_z.at[source], z_send.at[0], z_recv.at[source], blk=other).wait_recv()
        total = total + recv_z[source].astype(F32)
    scale = lax.rsqrt(jnp.mean(total * total, axis=-1, keepdims=True) + EPS)
    out_ref[...] = (mid_ref[...].astype(F32) + total * scale * gain_ref[1:2, :]).astype(BF16)

    for origin in range(lines):
        index = origin * 2 + x
        pass_on(index, 0, other).wait_send()

        @pl.when((origin <= z) & (z < lines - 1))
        def _():
            pass_on(index, 1, me + 2).wait_send()

        @pl.when((origin >= z) & (z > 0))
        def _():
            pass_on(index, 2, me - 2).wait_send()

        @pl.when(origin != z)
        def _():
            to_z(origin).wait_send()


def layer_kernel(
    spread_count,
    states_ref, wqkv_hbm, gain_ref, wout_hbm, post_ref, wgu_hbm, wd_hbm, keys_hbm, values_hbm,
    slot_node, node_length, node_parent, segment_ref, leaf_node, frequency_ref, out_ref,
    wqkv, wout, raw, query, key, value, squares, query_in, keys_in, values_in,
    cos_ref, sin_ref, limits, own_info,
    peak, norm, acc, leaf_peak, leaf_norm, leaf_acc, part_out, part_in, stat_out, stat_in,
    attended, proj, proj_low, pair_in, pair_out, line_in, mid_ref,
    gathered, wgu, wd, hidden, whole, own_part, own_sum, send_x, recv_x, recv_z,
    w_sem, s_send, s_recv, q_send, q_recv, own_sem, k_send, k_recv, v_send, v_recv,
    p_send, p_recv, t_send, t_recv, c_send, c_recv, y_send, y_recv,
    g_send, g_recv, x_send, x_recv, z_send, z_recv,
):
    rows, width = states_ref.shape
    heads = query.shape[0]
    node_rows = keys_hbm.shape[1]
    slots = slot_node.shape[0]
    me = lax.axis_index("blk")
    head = lax.axis_index("head")
    mine, rest = me // spread_count, me % spread_count
    scale = HD ** (-0.5)

    loads = [pltpu.make_async_copy(wqkv_hbm.at[c], wqkv.at[c], w_sem.at[c]) for c in range(3)]
    loads.append(pltpu.make_async_copy(wout_hbm, wout, w_sem.at[3]))
    late = [
        pltpu.make_async_copy(wgu_hbm.at[0], wgu.at[0], w_sem.at[4]),
        pltpu.make_async_copy(wgu_hbm.at[1], wgu.at[1], w_sem.at[5]),
        pltpu.make_async_copy(wd_hbm, wd, w_sem.at[6]),
    ]
    for load in loads:
        load.start()

    def holder(index):
        return index * spread_count + rest

    peers = [{"head": (head + j) % 4} for j in range(1, 4)]
    peers += [{"blk": holder((mine + j) % heads)} for j in range(1, heads)]
    peers += [{"blk": mine * spread_count + (rest + j) % spread_count} for j in range(1, spread_count)]
    lines = slots // 2
    if spread_count != 2:
        peers += [{"blk": me // 2 * 2 + 1 - me % 2}]
        peers += [{"blk": (me // 2 + j) % lines * 2 + me % 2} for j in range(1, lines)]
    meet(peers)

    def column(index):
        return pl.ds(pl.multiple_of(index * HD, HD), HD)

    def place(buffer, index, member):
        return buffer.at[member, pl.ds(pl.multiple_of(index * node_rows, node_rows), node_rows)]

    def cache_out(target):
        return (
            remote(keys_hbm.at[0, :, column(target)], place(keys_in, mine, rest), k_send.at[0, target], k_recv.at[mine, rest], blk=holder(target)),
            remote(values_hbm.at[0, :, column(target)], place(values_in, mine, rest), v_send.at[0, target], v_recv.at[mine, rest], blk=holder(target)),
        )

    def cache_wait(source, member):
        far = holder((mine + 1) % heads)
        spot, spot_too = place(keys_in, source, member), place(values_in, source, member)
        remote(spot, spot, k_send.at[0, 0], k_recv.at[source, member], blk=far).wait_recv()
        remote(spot_too, spot_too, v_send.at[0, 0], v_recv.at[source, member], blk=far).wait_recv()

    def cache_on(source, j, own):
        target = mine * spread_count + (rest + j) % spread_count
        spot, spot_too = place(keys_in, source, rest), place(values_in, source, rest)
        from_keys = keys_hbm.at[0, :, column(mine)] if own else spot
        from_values = values_hbm.at[0, :, column(mine)] if own else spot_too
        return (
            remote(from_keys, spot, k_send.at[j, source], k_recv.at[source, rest], blk=target),
            remote(from_values, spot_too, v_send.at[j, source], v_recv.at[source, rest], blk=target),
        )

    for j in range(1, heads):
        for copy in cache_out((mine + j) % heads):
            copy.start()
    for j in range(1, spread_count):
        for copy in cache_on(mine, j, True):
            copy.start()
    own_copies = [
        pltpu.make_async_copy(keys_hbm.at[0, :, column(mine)], place(keys_in, mine, rest), own_sem.at[0]),
        pltpu.make_async_copy(values_hbm.at[0, :, column(mine)], place(values_in, mine, rest), own_sem.at[1]),
    ]
    for copy in own_copies:
        copy.start()

    def pass_on(step):
        source = by_distance(mine, heads, step)
        cache_wait(source, rest)
        for j in range(1, spread_count):
            for copy in cache_on(source, j, False):
                copy.start()

    leaves, middles, nodes = leaf_node.shape[1], node_parent.shape[0], node_length.shape[0]

    def upright(lines_of):
        filled = HD - len(lines_of)
        return jnp.transpose(jnp.concatenate(lines_of + [jnp.zeros((filled, rows), F32)], axis=0))

    def seen_by(group):
        segment = segment_ref[pl.ds(group, 1), :]
        middle, root = jnp.zeros_like(segment), jnp.zeros_like(segment)
        for leaf in range(leaves):
            middle = jnp.where(segment == leaf, leaf_node[group, leaf], middle)
        for index in range(middles):
            root = jnp.where(middle == nodes - middles + index, node_parent[index], root)
        middle_rows, root_rows = jnp.zeros_like(segment), jnp.zeros_like(segment)
        for node in range(nodes):
            middle_rows = jnp.where(middle == node, node_length[node], middle_rows)
            root_rows = jnp.where(root == node, node_length[node], root_rows)
        return segment, middle, root, middle_rows, root_rows

    for g in range(heads):
        _, middle, root, middle_rows, root_rows = seen_by(holder(g))
        lines_of = []
        for j in range(spread_count):
            for index in range(heads):
                node = slot_node[index * spread_count + (rest + j) % spread_count]
                row = jnp.where(middle == node, middle_rows, jnp.where(root == node, root_rows, 0))
                lines_of.append(row.astype(F32))
        limits[g] = upright(lines_of)
    segment, _, _, middle_rows, root_rows = seen_by(me)
    first = jnp.zeros_like(segment)
    start = jnp.zeros((1, 1), F32)
    first = jnp.zeros(segment.shape, F32)
    for leaf in range(leaves):
        inside = (segment == leaf).astype(F32)
        first = first + inside * start
        start = start + jnp.sum(inside, axis=-1, keepdims=True)
    token = lax.broadcasted_iota(jnp.int32, (1, rows), 1)
    position = (middle_rows + root_rows + token).astype(F32) - first
    own_info[...] = upright([first, position])

    tile = 2 * HD
    here = heads * HD

    def product(c):
        loads[c].wait()

        @pl.loop(0, here // tile)
        def _(t):
            at = pl.ds(pl.multiple_of(t * tile, tile), tile)
            raw[c, :, at] = jnp.dot(states_ref[...], wqkv[c, :, at], preferred_element_type=F32)

    lane = lax.broadcasted_iota(jnp.int32, (rows, HD), 1)
    product(0)
    product(1)
    query_sum = jnp.sum(raw[0] * raw[0], axis=-1, keepdims=True)
    key_sum = jnp.sum(raw[1] * raw[1], axis=-1, keepdims=True)
    packed = jnp.where(lane == 0, query_sum, jnp.where(lane == 1, key_sum, 0.0))
    squares[head] = jnp.transpose(packed)[0:8]

    def squares_to(target):
        return remote(squares.at[head], squares.at[head], s_send.at[target], s_recv.at[head], head=target)

    for j in range(1, 4):
        squares_to((head + j) % 4).start()
    pass_on(1)
    product(2)
    for load in late:
        load.start()
    value[...] = raw[2].astype(BF16)
    pass_on(2)
    angles = own_info[:, 1:2] * frequency_ref[...]
    cos_ref[...] = jnp.cos(angles)
    sines = jnp.sin(angles)
    sin_ref[...] = jnp.where(lane < HD // 2, -sines, sines)
    total = squares[head]
    for j in range(1, 4):
        source = (head + j) % 4
        remote(squares.at[source], squares.at[source], s_send.at[source], s_recv.at[source], head=source).wait_recv()
        total = total + squares[source]
    spread = jnp.transpose(jnp.concatenate([total] * (HD // 8), axis=0))
    scales = lax.rsqrt(spread / width + EPS)
    query_scale, key_scale = scales[:, 0:1], scales[:, 1:2]

    def turned(c, h, by):
        at = slice(h * HD, (h + 1) * HD)
        normed = raw[c, :, at] * by * gain_ref[c : c + 1, at]
        swapped = pltpu.roll(normed, HD // 2, 1)
        return (normed * cos_ref[...] + swapped * sin_ref[...]).astype(BF16)

    for h in range(heads):
        query[h] = turned(0, h, query_scale)

    def query_to(target):
        return remote(query.at[target], query_in.at[mine], q_send.at[target], q_recv.at[mine], blk=holder(target))

    for j in range(1, heads):
        query_to((mine + j) % heads).start()
    query_in[mine] = query[mine]
    for h in range(heads):
        key[h] = turned(1, h, key_scale)
    for step in range(3, heads):
        pass_on(step)

    row_at = lax.broadcasted_iota(jnp.int32, (rows, rows), 0)
    key_at = lax.broadcasted_iota(jnp.int32, (rows, rows), 1)
    see_leaf = (key_at.astype(F32) >= own_info[:, 0:1]) & (key_at <= row_at)
    over = (((1,), (1,)), ((), ()))
    for h in range(heads):
        scores = lax.dot_general(query[h], key[h], over, preferred_element_type=F32) * scale
        scores = jnp.where(see_leaf, scores, NEG)
        top = jnp.max(scores, axis=-1, keepdims=True)
        weights = jnp.exp(scores - top)
        leaf_peak[h] = jnp.broadcast_to(top, (rows, HD))
        leaf_norm[h] = jnp.broadcast_to(jnp.sum(weights, axis=-1, keepdims=True), (rows, HD))
        leaf_acc[h] = jnp.dot(weights.astype(BF16), value[:, h * HD : (h + 1) * HD], preferred_element_type=F32)

    for j in range(1, heads):
        source = (mine + j) % heads
        remote(query.at[0], query_in.at[source], q_send.at[0], q_recv.at[source], blk=holder(source)).wait_recv()
    key_row = lax.broadcasted_iota(jnp.int32, (rows, node_rows), 1).astype(F32)

    def part_to(target):
        return (
            remote(part_out.at[target], part_in.at[mine], p_send.at[target], p_recv.at[mine], blk=holder(target)),
            remote(stat_out.at[target], stat_in.at[mine], t_send.at[target], t_recv.at[mine], blk=holder(target)),
        )

    for copy in own_copies:
        copy.wait()
    for j in range(spread_count):
        member = (rest + j) % spread_count
        if j > 0:
            for step in range(heads):
                cache_wait(by_distance(mine, heads, step), member)

        @pl.loop(0, heads)
        def _(turn):
            g = (mine + 1 + turn) % heads
            scores = lax.dot_general(query_in[g], keys_in[member], over, preferred_element_type=F32) * scale
            limit = limits[g]
            masked = [
                jnp.where(
                    key_row < limit[:, j * heads + index : j * heads + index + 1],
                    scores[:, index * node_rows : (index + 1) * node_rows],
                    NEG,
                )
                for index in range(heads)
            ]
            highest = functools.reduce(jnp.maximum, masked)
            top = jnp.max(highest, axis=-1, keepdims=True)
            if j > 0:
                top = jnp.maximum(top, peak[g][:, 0:1])
            weights = [jnp.exp(part - top) for part in masked]
            total = jnp.sum(functools.reduce(jnp.add, weights), axis=-1, keepdims=True)
            summed = jnp.dot(
                jnp.concatenate([part.astype(BF16) for part in weights], axis=-1),
                values_in[member],
                preferred_element_type=F32,
            )
            if j > 0:
                shrink = jnp.exp(peak[g][:, 0:1] - top)
                total = total + norm[g][:, 0:1] * shrink
                summed = summed + acc[g] * shrink
            if j < spread_count - 1:
                peak[g] = jnp.broadcast_to(top, (rows, HD))
                norm[g] = jnp.broadcast_to(total, (rows, HD))
                acc[g] = summed
            else:
                part_out[g] = (summed / total).astype(BF16)
                stats = jnp.where(lane == 0, top, jnp.where(lane == 1, total, 0.0))
                stat_out[g] = jnp.transpose(stats)[0:8]

                @pl.when(turn < heads - 1)
                def _():
                    for copy in part_to(g):
                        copy.start()

    part_in[mine] = part_out[mine]
    stat_in[mine] = stat_out[mine]
    for j in range(1, heads):
        source = (mine + j) % heads
        remote(part_out.at[0], part_in.at[source], p_send.at[0], p_recv.at[source], blk=holder(source)).wait_recv()
        remote(stat_out.at[0], stat_in.at[source], t_send.at[0], t_recv.at[source], blk=holder(source)).wait_recv()
    for h in range(heads):
        stats = jnp.transpose(jnp.concatenate([stat_in[h]] * (HD // 8), axis=0))
        other_peak, other_norm = stats[:, 0:1], stats[:, 1:2]
        top = jnp.maximum(leaf_peak[h], other_peak)
        own_scale = jnp.exp(leaf_peak[h] - top)
        other_scale = jnp.exp(other_peak - top) * other_norm
        summed = leaf_acc[h] * own_scale + part_in[h].astype(F32) * other_scale
        attended[:, h * HD : (h + 1) * HD] = (
            summed / (leaf_norm[h] * own_scale + other_scale)
        ).astype(BF16)

    loads[3].wait()
    y, core = head // 2, head % 2
    own_rows = out_ref.shape[0]
    sibling, across = y * 2 + 1 - core, (1 - y) * 2 + core
    tiles = c_send.shape[1]
    wide = width // tiles

    def rows_of(index):
        return pl.ds(pl.multiple_of(index * own_rows, own_rows), own_rows)

    def cols_of(t):
        return pl.ds(t * wide, wide)

    def to_pair(half, t):
        return remote(
            proj_low.at[rows_of(half * 2 + 1 - core), cols_of(t)],
            pair_in.at[half, :, cols_of(t)],
            c_send.at[half, t], c_recv.at[half, t], head=sibling,
        )

    def to_line(t):
        return remote(pair_out.at[:, cols_of(t)], line_in.at[:, cols_of(t)], y_send.at[t], y_recv.at[t], head=across)

    def on_line(t):
        to_pair(1 - y, t).wait_recv()
        pair_out[:, cols_of(t)] = (
            proj[rows_of(across), cols_of(t)] + pair_in[1 - y, :, cols_of(t)].astype(F32)
        ).astype(BF16)
        to_line(t).start()

    for t in range(tiles):
        tiled = jnp.dot(attended[...], wout[:, cols_of(t)], preferred_element_type=F32)
        proj[:, cols_of(t)] = tiled
        proj_low[:, cols_of(t)] = tiled.astype(BF16)
        to_pair(1 - y, t).start()
        to_pair(y, t).start()
        if t > 0:
            on_line(t - 1)
    on_line(tiles - 1)
    for t in range(tiles):
        to_pair(y, t).wait_recv()
        to_line(t).wait_recv()
    total = proj[rows_of(head), :] + pair_in[y].astype(F32) + line_in[...].astype(F32)
    shrink = lax.rsqrt(jnp.mean(total * total, axis=-1, keepdims=True) + EPS)
    own = states_ref[rows_of(head), :].astype(F32)
    mid_ref[...] = (own + total * shrink * post_ref[0:1, :]).astype(BF16)

    mlp_part(
        lines, late,
        mid_ref, post_ref, out_ref,
        gathered, wgu, wd, hidden, whole, own_part, own_sum, send_x, recv_x, recv_z,
        g_send, g_recv, x_send, x_recv, z_send, z_recv,
    )

    for t in range(tiles):
        to_line(t).wait_send()
        for half in range(2):
            to_pair(half, t).wait_send()
    for j in range(1, 4):
        squares_to((head + j) % 4).wait_send()
    for j in range(1, heads):
        target = (mine + j) % heads
        query_to(target).wait_send()
        for copy in cache_out(target) + part_to(target):
            copy.wait_send()
    for source in range(heads):
        for j in range(1, spread_count):
            for copy in cache_on(source, j, False):
                copy.wait_send()


def on_device(
    states_in,
    w_qkv,
    qk_gain,
    w_out,
    post_gain,
    w_gate_up,
    w_down,
    cache_keys,
    cache_values,
    slot_node,
    node_length,
    node_parent,
    leaf_segment,
    leaf_node,
):
    rows, width = states_in.shape
    here = w_qkv.shape[2]
    heads = here // HD
    node_rows = cache_keys.shape[1]
    own_rows = rows // 4
    units = w_down.shape[0]
    slots = slot_node.shape[0]
    spread_count = slots // heads
    lines = slots // 2
    tiles = 4
    vmem = pl.BlockSpec(memory_space=pltpu.VMEM)
    smem = pl.BlockSpec(memory_space=pltpu.SMEM)
    hbm = pl.BlockSpec(memory_space=pl.ANY)
    dma = pltpu.SemaphoreType.DMA
    half = HD // 2
    frequency = THETA ** (-2.0 * jnp.arange(half, dtype=F32) / HD)

    def per_head(kind):
        return pltpu.VMEM((heads, rows, HD), kind)

    cached = pltpu.VMEM((spread_count, heads * node_rows, HD), BF16)
    part = pltpu.VMEM((lines, own_rows, width), BF16)
    return pl.pallas_call(
        functools.partial(layer_kernel, spread_count),
        out_shape=jax.ShapeDtypeStruct((own_rows, width), BF16),
        in_specs=[vmem, hbm, vmem, hbm, vmem, hbm, hbm, hbm, hbm, smem, smem, smem, vmem, smem, vmem],
        out_specs=vmem,
        scratch_shapes=[
            pltpu.VMEM(w_qkv.shape, BF16),
            pltpu.VMEM(w_out.shape, BF16),
            pltpu.VMEM((3, rows, here), F32),
            per_head(BF16),
            per_head(BF16),
            pltpu.VMEM((rows, here), BF16),
            pltpu.VMEM((4, 8, rows), F32),
            per_head(BF16),
            cached,
            cached,
            pltpu.VMEM((rows, HD), F32),
            pltpu.VMEM((rows, HD), F32),
            per_head(F32),
            pltpu.VMEM((rows, HD), F32),
            per_head(F32), per_head(F32), per_head(F32),
            per_head(F32), per_head(F32), per_head(F32),
            per_head(BF16), per_head(BF16),
            pltpu.VMEM((heads, 8, rows), F32),
            pltpu.VMEM((heads, 8, rows), F32),
            pltpu.VMEM((rows, here), BF16),
            pltpu.VMEM((rows, width), F32),
            pltpu.VMEM((rows, width), BF16),
            pltpu.VMEM((2, own_rows, width), BF16),
            pltpu.VMEM((own_rows, width), BF16),
            pltpu.VMEM((own_rows, width), BF16),
            pltpu.VMEM((own_rows, width), BF16),
            pltpu.VMEM((slots * own_rows, width), BF16),
            pltpu.VMEM(w_gate_up.shape, BF16),
            pltpu.VMEM(w_down.shape, BF16),
            pltpu.VMEM((2 * own_rows, units), BF16),
            pltpu.VMEM((2 * own_rows, width), F32),
            pltpu.VMEM((2, own_rows, width), F32),
            pltpu.VMEM((own_rows, width), F32),
            part, part, part,
            dma((7,)),
            dma((4,)), dma((4,)),
            dma((heads,)), dma((heads,)),
            dma((2,)),
            dma((spread_count, heads)), dma((heads, spread_count)),
            dma((spread_count, heads)), dma((heads, spread_count)),
            dma((heads,)), dma((heads,)),
            dma((heads,)), dma((heads,)),
            dma((2, tiles)), dma((2, tiles)),
            dma((tiles,)), dma((tiles,)),
            dma((3, slots)),
            dma((slots,)),
            dma((lines,)), dma((lines,)),
            dma((lines,)), dma((lines,)),
        ],
        compiler_params=pltpu.CompilerParams(
            collective_id=1, has_side_effects=True, vmem_limit_bytes=62 * 2**20
        ),
    )(
        states_in, w_qkv, qk_gain, w_out, post_gain, w_gate_up, w_down, cache_keys, cache_values,
        slot_node, node_length, node_parent, leaf_segment, leaf_node,
        jnp.concatenate([frequency, frequency])[None, :],
    )


def solution(mesh):
    placed = (
        P("blk", None),
        P(None, None, "head"),
        P(None, "head"),
        P("head", None),
        P(),
        P(None, None, "blk"),
        P("blk", None),
        P("blk", None, "head"),
        P("blk", None, "head"),
        P(),
        P(),
        P(),
        P(),
        P(),
    )
    return jax.shard_map(
        on_device, mesh=mesh, in_specs=placed, out_specs=P(("blk", "head"), None), check_vma=False
    )
```

```python
import functools

import jax
import jax.numpy as jnp
from jax import lax
from jax.experimental import pallas as pl
from jax.experimental.pallas import tpu as pltpu
from jax.sharding import PartitionSpec as P

HD = 128
EPS = 1e-06
THETA = 500000.0
NEG = -1e30
MESH = pl.DeviceIdType.MESH
BF16 = jnp.bfloat16
F32 = jnp.float32


def by_distance(at, count, step):
    back = count - 1 - at
    near = jnp.minimum(at, back)
    both = jnp.where(step % 2 == 1, at - (step + 1) // 2, at + step // 2)
    return jnp.where(step <= 2 * near, both, jnp.where(at < back, step, count - 1 - step))


def remote(src, dst, send_sem, recv_sem, **where):
    return pltpu.make_async_remote_copy(
        src_ref=src,
        dst_ref=dst,
        send_sem=send_sem,
        recv_sem=recv_sem,
        device_id=where,
        device_id_type=MESH,
    )


def meet(peers):
    barrier = pltpu.get_barrier_semaphore()
    for peer in peers:
        pl.semaphore_signal(barrier, inc=1, device_id=peer, device_id_type=MESH)
    return lambda: pl.semaphore_wait(barrier, len(peers))


def mlp_part(
    lines, loads,
    mid_ref, gain_ref, out_ref,
    gathered, wgu, wd, hidden, whole, own_part, own_sum, send_x, recv_x, recv_z,
    g_send, g_recv, x_send, x_recv, z_send, z_recv,
):
    rows, width = mid_ref.shape
    units = wd.shape[0]
    me = lax.axis_index("blk")
    z, x = me // 2, me % 2
    other = z * 2 + 1 - x

    def block(index):
        return gathered.at[pl.ds(pl.multiple_of(index * rows, rows), rows)]

    def pass_on(index, way, target):
        return remote(block(index), block(index), g_send.at[way, index], g_recv.at[index], blk=target)

    def spread(origin, wait):
        index = origin * 2 + x
        if wait:
            pass_on(index, 0, other).wait_recv()
        pass_on(index, 0, other).start()

        @pl.when((origin <= z) & (z < lines - 1))
        def _():
            pass_on(index, 1, me + 2).start()

        @pl.when((origin >= z) & (z > 0))
        def _():
            pass_on(index, 2, me - 2).start()

    gathered[pl.ds(pl.multiple_of(me * rows, rows), rows), :] = mid_ref[...]
    spread(z, False)

    tiles = x_send.shape[1]
    wide = width // tiles

    def cols_of(t):
        return pl.ds(pl.multiple_of(t * wide, wide), wide)

    def to_x(origin, t):
        return remote(
            send_x.at[origin, :, cols_of(t)], recv_x.at[origin, :, cols_of(t)],
            x_send.at[origin, t], x_recv.at[origin, t], blk=other,
        )

    def to_z(origin, t):
        return remote(
            send_x.at[origin, :, cols_of(t)], recv_z.at[z, :, cols_of(t)],
            z_send.at[origin, t], z_recv.at[z, t], blk=origin * 2 + x,
        )

    def reduce_x(step):
        origin = by_distance(z, lines, step)

        @pl.loop(0, tiles)
        def _(t):
            at = cols_of(t)
            to_x(origin, t).wait_recv()
            summed = own_part[step % 2, :, at] + recv_x[origin, :, at].astype(F32)
            to_x(origin, t).wait_send()
            if step == 0:
                own_sum[:, at] = summed
            else:
                send_x[origin, :, at] = summed.astype(BF16)
                to_z(origin, t).start()

    tile = min(256, units)
    for step in range(lines):
        origin = by_distance(z, lines, step)
        if step + 1 < lines:
            spread(by_distance(z, lines, step + 1), True)
        pass_on(origin * 2 + 1 - x, 0, other).wait_recv()
        if step == 0:
            loads[0].wait()
            loads[1].wait()
        chunk = pl.ds(pl.multiple_of(origin * 2 * rows, 2 * rows), 2 * rows)

        @pl.loop(0, units // tile)
        def _(t):
            at = pl.ds(pl.multiple_of(t * tile, tile), tile)
            state = gathered[chunk, :]
            gate = jnp.dot(state, wgu[0, :, at], preferred_element_type=F32)
            up = jnp.dot(state, wgu[1, :, at], preferred_element_type=F32)
            hidden[:, at] = (gate / (1.0 + jnp.exp(-gate)) * up).astype(BF16)

        if step == 0:
            loads[2].wait()

        @pl.loop(0, tiles)
        def _(t):
            at = cols_of(t)
            whole[:, at] = jnp.dot(hidden[...], wd[:, at], preferred_element_type=F32)
            own_part[step % 2, :, at] = whole[pl.ds(pl.multiple_of(x * rows, rows), rows), at]
            send_x[origin, :, at] = whole[
                pl.ds(pl.multiple_of((1 - x) * rows, rows), rows), at
            ].astype(BF16)
            to_x(origin, t).start()

        if step > 0:
            reduce_x(step - 1)
    reduce_x(lines - 1)

    total = own_sum[...]
    for j in range(1, lines):
        source = (z + j) % lines
        for t in range(tiles):
            spot = recv_z.at[source, :, cols_of(t)]
            remote(spot, spot, z_send.at[0, t], z_recv.at[source, t], blk=other).wait_recv()
        total = total + recv_z[source].astype(F32)
    scale = lax.rsqrt(jnp.mean(total * total, axis=-1, keepdims=True) + EPS)
    out_ref[...] = (mid_ref[...].astype(F32) + total * scale * gain_ref[1:2, :]).astype(BF16)

    for origin in range(lines):
        index = origin * 2 + x
        pass_on(index, 0, other).wait_send()

        @pl.when((origin <= z) & (z < lines - 1))
        def _():
            pass_on(index, 1, me + 2).wait_send()

        @pl.when((origin >= z) & (z > 0))
        def _():
            pass_on(index, 2, me - 2).wait_send()

        @pl.when(origin != z)
        def _():
            for t in range(tiles):
                to_z(origin, t).wait_send()


def layer_kernel(
    spread_count,
    states_ref, wqkv_hbm, gain_ref, wout_hbm, post_ref, wgu_hbm, wd_hbm, keys_hbm, values_hbm,
    slot_node, node_length, node_parent, segment_ref, leaf_node, frequency_ref, out_ref,
    wqkv, wout, raw, query, key, value, squares, query_in, keys_in, values_in,
    cos_ref, sin_ref, limits, own_info,
    peak, norm, acc, leaf_peak, leaf_norm, leaf_acc, part_out, part_in, stat_out, stat_in,
    attended, proj, proj_low, pair_in, pair_out, line_in, mid_ref,
    gathered, wgu, wd, hidden, whole, own_part, own_sum, send_x, recv_x, recv_z,
    w_sem, s_send, s_recv, q_send, q_recv, own_sem, k_send, k_recv, v_send, v_recv,
    p_send, p_recv, t_send, t_recv, c_send, c_recv, y_send, y_recv,
    g_send, g_recv, x_send, x_recv, z_send, z_recv,
):
    rows, width = states_ref.shape
    heads = query.shape[0]
    node_rows = keys_hbm.shape[1]
    slots = slot_node.shape[0]
    me = lax.axis_index("blk")
    head = lax.axis_index("head")
    mine, rest = me // spread_count, me % spread_count
    scale = HD ** (-0.5)

    loads = [pltpu.make_async_copy(wqkv_hbm.at[c], wqkv.at[c], w_sem.at[c]) for c in range(3)]
    loads.append(pltpu.make_async_copy(wout_hbm, wout, w_sem.at[3]))
    late = [
        pltpu.make_async_copy(wgu_hbm.at[0], wgu.at[0], w_sem.at[4]),
        pltpu.make_async_copy(wgu_hbm.at[1], wgu.at[1], w_sem.at[5]),
        pltpu.make_async_copy(wd_hbm, wd, w_sem.at[6]),
    ]
    for load in loads:
        load.start()

    def holder(index):
        return index * spread_count + rest

    peers = [{"head": (head + j) % 4} for j in range(1, 4)]
    peers += [{"blk": holder((mine + j) % heads)} for j in range(1, heads)]
    peers += [{"blk": mine * spread_count + (rest + j) % spread_count} for j in range(1, spread_count)]
    lines = slots // 2
    if spread_count != 2:
        peers += [{"blk": me // 2 * 2 + 1 - me % 2}]
        peers += [{"blk": (me // 2 + j) % lines * 2 + me % 2} for j in range(1, lines)]
    all_here = meet(peers)

    def column(index):
        return pl.ds(pl.multiple_of(index * HD, HD), HD)

    def place(buffer, index, member):
        return buffer.at[member, pl.ds(pl.multiple_of(index * node_rows, node_rows), node_rows)]

    def cache_out(target):
        return (
            remote(keys_hbm.at[0, :, column(target)], place(keys_in, mine, rest), k_send.at[0, target], k_recv.at[mine, rest], blk=holder(target)),
            remote(values_hbm.at[0, :, column(target)], place(values_in, mine, rest), v_send.at[0, target], v_recv.at[mine, rest], blk=holder(target)),
        )

    def cache_wait(source, member):
        far = holder((mine + 1) % heads)
        spot, spot_too = place(keys_in, source, member), place(values_in, source, member)
        remote(spot, spot, k_send.at[0, 0], k_recv.at[source, member], blk=far).wait_recv()
        remote(spot_too, spot_too, v_send.at[0, 0], v_recv.at[source, member], blk=far).wait_recv()

    def cache_on(source, j, own):
        target = mine * spread_count + (rest + j) % spread_count
        spot, spot_too = place(keys_in, source, rest), place(values_in, source, rest)
        from_keys = keys_hbm.at[0, :, column(mine)] if own else spot
        from_values = values_hbm.at[0, :, column(mine)] if own else spot_too
        return (
            remote(from_keys, spot, k_send.at[j, source], k_recv.at[source, rest], blk=target),
            remote(from_values, spot_too, v_send.at[j, source], v_recv.at[source, rest], blk=target),
        )

    own_copies = [
        pltpu.make_async_copy(keys_hbm.at[0, :, column(mine)], place(keys_in, mine, rest), own_sem.at[0]),
        pltpu.make_async_copy(values_hbm.at[0, :, column(mine)], place(values_in, mine, rest), own_sem.at[1]),
    ]
    for copy in own_copies:
        copy.start()

    def pass_on(step):
        source = by_distance(mine, heads, step)
        cache_wait(source, rest)
        for j in range(1, spread_count):
            for copy in cache_on(source, j, False):
                copy.start()

    leaves, middles, nodes = leaf_node.shape[1], node_parent.shape[0], node_length.shape[0]

    def upright(lines_of):
        filled = HD - len(lines_of)
        return jnp.transpose(jnp.concatenate(lines_of + [jnp.zeros((filled, rows), F32)], axis=0))

    def seen_by(group):
        segment = segment_ref[pl.ds(group, 1), :]
        middle, root = jnp.zeros_like(segment), jnp.zeros_like(segment)
        for leaf in range(leaves):
            middle = jnp.where(segment == leaf, leaf_node[group, leaf], middle)
        for index in range(middles):
            root = jnp.where(middle == nodes - middles + index, node_parent[index], root)
        middle_rows, root_rows = jnp.zeros_like(segment), jnp.zeros_like(segment)
        for node in range(nodes):
            middle_rows = jnp.where(middle == node, node_length[node], middle_rows)
            root_rows = jnp.where(root == node, node_length[node], root_rows)
        return segment, middle, root, middle_rows, root_rows

    for g in range(heads):
        _, middle, root, middle_rows, root_rows = seen_by(holder(g))
        lines_of = []
        for j in range(spread_count):
            for index in range(heads):
                node = slot_node[index * spread_count + (rest + j) % spread_count]
                row = jnp.where(middle == node, middle_rows, jnp.where(root == node, root_rows, 0))
                lines_of.append(row.astype(F32))
        limits[g] = upright(lines_of)
    segment, _, _, middle_rows, root_rows = seen_by(me)
    first = jnp.zeros(segment.shape, F32)
    start = jnp.zeros((1, 1), F32)
    for leaf in range(leaves):
        inside = (segment == leaf).astype(F32)
        first = first + inside * start
        start = start + jnp.sum(inside, axis=-1, keepdims=True)
    token = lax.broadcasted_iota(jnp.int32, (1, rows), 1)
    position = (middle_rows + root_rows + token).astype(F32) - first
    own_info[...] = upright([first, position])

    all_here()
    for j in range(1, heads):
        for copy in cache_out((mine + j) % heads):
            copy.start()
    for j in range(1, spread_count):
        for copy in cache_on(mine, j, True):
            copy.start()

    tile = 2 * HD
    here = heads * HD

    def product(c):
        loads[c].wait()

        @pl.loop(0, here // tile)
        def _(t):
            at = pl.ds(pl.multiple_of(t * tile, tile), tile)
            raw[c, :, at] = jnp.dot(states_ref[...], wqkv[c, :, at], preferred_element_type=F32)

    lane = lax.broadcasted_iota(jnp.int32, (rows, HD), 1)
    product(0)
    product(1)
    query_sum = jnp.sum(raw[0] * raw[0], axis=-1, keepdims=True)
    key_sum = jnp.sum(raw[1] * raw[1], axis=-1, keepdims=True)
    packed = jnp.where(lane == 0, query_sum, jnp.where(lane == 1, key_sum, 0.0))
    squares[head] = jnp.transpose(packed)[0:8]

    def squares_to(target):
        return remote(squares.at[head], squares.at[head], s_send.at[target], s_recv.at[head], head=target)

    for j in range(1, 4):
        squares_to((head + j) % 4).start()
    product(2)
    for load in late:
        load.start()
    value[...] = raw[2].astype(BF16)
    angles = own_info[:, 1:2] * frequency_ref[...]
    cos_ref[...] = jnp.cos(angles)
    sines = jnp.sin(angles)
    sin_ref[...] = jnp.where(lane < HD // 2, -sines, sines)
    total = squares[head]
    for j in range(1, 4):
        source = (head + j) % 4
        remote(squares.at[source], squares.at[source], s_send.at[source], s_recv.at[source], head=source).wait_recv()
        total = total + squares[source]
    spread = jnp.transpose(jnp.concatenate([total] * (HD // 8), axis=0))
    scales = lax.rsqrt(spread / width + EPS)
    query_scale, key_scale = scales[:, 0:1], scales[:, 1:2]

    def turned(c, h, by):
        at = slice(h * HD, (h + 1) * HD)
        normed = raw[c, :, at] * by * gain_ref[c : c + 1, at]
        swapped = pltpu.roll(normed, HD // 2, 1)
        return (normed * cos_ref[...] + swapped * sin_ref[...]).astype(BF16)

    for h in range(heads):
        query[h] = turned(0, h, query_scale)

    def query_to(target):
        return remote(query.at[target], query_in.at[mine], q_send.at[target], q_recv.at[mine], blk=holder(target))

    for j in range(1, heads):
        query_to((mine + j) % heads).start()
    query_in[mine] = query[mine]
    for step in range(1, heads):
        pass_on(step)
    for h in range(heads):
        key[h] = turned(1, h, key_scale)

    row_at = lax.broadcasted_iota(jnp.int32, (rows, rows), 0)
    key_at = lax.broadcasted_iota(jnp.int32, (rows, rows), 1)
    see_leaf = (key_at.astype(F32) >= own_info[:, 0:1]) & (key_at <= row_at)
    over = (((1,), (1,)), ((), ()))
    for h in range(heads):
        scores = lax.dot_general(query[h], key[h], over, preferred_element_type=F32) * scale
        scores = jnp.where(see_leaf, scores, NEG)
        top = jnp.max(scores, axis=-1, keepdims=True)
        weights = jnp.exp(scores - top)
        leaf_peak[h] = jnp.broadcast_to(top, (rows, HD))
        leaf_norm[h] = jnp.broadcast_to(jnp.sum(weights, axis=-1, keepdims=True), (rows, HD))
        leaf_acc[h] = jnp.dot(weights.astype(BF16), value[:, h * HD : (h + 1) * HD], preferred_element_type=F32)

    for j in range(1, heads):
        source = (mine + j) % heads
        remote(query.at[0], query_in.at[source], q_send.at[0], q_recv.at[source], blk=holder(source)).wait_recv()
    key_row = lax.broadcasted_iota(jnp.int32, (rows, node_rows), 1).astype(F32)

    def part_to(target):
        return (
            remote(part_out.at[target], part_in.at[mine], p_send.at[target], p_recv.at[mine], blk=holder(target)),
            remote(stat_out.at[target], stat_in.at[mine], t_send.at[target], t_recv.at[mine], blk=holder(target)),
        )

    for copy in own_copies:
        copy.wait()
    for j in range(spread_count):
        member = (rest + j) % spread_count
        if j > 0:
            for step in range(heads):
                cache_wait(by_distance(mine, heads, step), member)

        @pl.loop(0, heads)
        def _(turn):
            g = (mine + 1 + turn) % heads
            scores = lax.dot_general(query_in[g], keys_in[member], over, preferred_element_type=F32) * scale
            limit = limits[g]
            masked = [
                jnp.where(
                    key_row < limit[:, j * heads + index : j * heads + index + 1],
                    scores[:, index * node_rows : (index + 1) * node_rows],
                    NEG,
                )
                for index in range(heads)
            ]
            highest = functools.reduce(jnp.maximum, masked)
            top = jnp.max(highest, axis=-1, keepdims=True)
            if j > 0:
                top = jnp.maximum(top, peak[g][:, 0:1])
            weights = [jnp.exp(part - top) for part in masked]
            total = jnp.sum(functools.reduce(jnp.add, weights), axis=-1, keepdims=True)
            summed = jnp.dot(
                jnp.concatenate([part.astype(BF16) for part in weights], axis=-1),
                values_in[member],
                preferred_element_type=F32,
            )
            if j > 0:
                shrink = jnp.exp(peak[g][:, 0:1] - top)
                total = total + norm[g][:, 0:1] * shrink
                summed = summed + acc[g] * shrink
            if j < spread_count - 1:
                peak[g] = jnp.broadcast_to(top, (rows, HD))
                norm[g] = jnp.broadcast_to(total, (rows, HD))
                acc[g] = summed
            else:
                part_out[g] = (summed / total).astype(BF16)
                stats = jnp.where(lane == 0, top, jnp.where(lane == 1, total, 0.0))
                stat_out[g] = jnp.transpose(stats)[0:8]

                @pl.when(turn < heads - 1)
                def _():
                    for copy in part_to(g):
                        copy.start()

    part_in[mine] = part_out[mine]
    stat_in[mine] = stat_out[mine]
    for j in range(1, heads):
        source = (mine + j) % heads
        remote(part_out.at[0], part_in.at[source], p_send.at[0], p_recv.at[source], blk=holder(source)).wait_recv()
        remote(stat_out.at[0], stat_in.at[source], t_send.at[0], t_recv.at[source], blk=holder(source)).wait_recv()
    for h in range(heads):
        stats = jnp.transpose(jnp.concatenate([stat_in[h]] * (HD // 8), axis=0))
        other_peak, other_norm = stats[:, 0:1], stats[:, 1:2]
        top = jnp.maximum(leaf_peak[h], other_peak)
        own_scale = jnp.exp(leaf_peak[h] - top)
        other_scale = jnp.exp(other_peak - top) * other_norm
        summed = leaf_acc[h] * own_scale + part_in[h].astype(F32) * other_scale
        attended[:, h * HD : (h + 1) * HD] = (
            summed / (leaf_norm[h] * own_scale + other_scale)
        ).astype(BF16)

    loads[3].wait()
    y, core = head // 2, head % 2
    own_rows = out_ref.shape[0]
    sibling, across = y * 2 + 1 - core, (1 - y) * 2 + core
    tiles = c_send.shape[1]
    wide = width // tiles

    def rows_of(index):
        return pl.ds(pl.multiple_of(index * own_rows, own_rows), own_rows)

    def cols_of(t):
        return pl.ds(t * wide, wide)

    def to_pair(half, t):
        return remote(
            proj_low.at[rows_of(half * 2 + 1 - core), cols_of(t)],
            pair_in.at[half, :, cols_of(t)],
            c_send.at[half, t], c_recv.at[half, t], head=sibling,
        )

    def to_line(t):
        return remote(pair_out.at[:, cols_of(t)], line_in.at[:, cols_of(t)], y_send.at[t], y_recv.at[t], head=across)

    def on_line(t):
        to_pair(1 - y, t).wait_recv()
        pair_out[:, cols_of(t)] = (
            proj[rows_of(across), cols_of(t)] + pair_in[1 - y, :, cols_of(t)].astype(F32)
        ).astype(BF16)
        to_line(t).start()

    for t in range(tiles):
        tiled = jnp.dot(attended[...], wout[:, cols_of(t)], preferred_element_type=F32)
        proj[:, cols_of(t)] = tiled
        proj_low[:, cols_of(t)] = tiled.astype(BF16)
        to_pair(1 - y, t).start()
        to_pair(y, t).start()
        if t > 0:
            on_line(t - 1)
    on_line(tiles - 1)
    for t in range(tiles):
        to_pair(y, t).wait_recv()
        to_line(t).wait_recv()
    total = proj[rows_of(head), :] + pair_in[y].astype(F32) + line_in[...].astype(F32)
    shrink = lax.rsqrt(jnp.mean(total * total, axis=-1, keepdims=True) + EPS)
    own = states_ref[rows_of(head), :].astype(F32)
    mid_ref[...] = (own + total * shrink * post_ref[0:1, :]).astype(BF16)

    mlp_part(
        lines, late,
        mid_ref, post_ref, out_ref,
        gathered, wgu, wd, hidden, whole, own_part, own_sum, send_x, recv_x, recv_z,
        g_send, g_recv, x_send, x_recv, z_send, z_recv,
    )

    for t in range(tiles):
        to_line(t).wait_send()
        for half in range(2):
            to_pair(half, t).wait_send()
    for j in range(1, 4):
        squares_to((head + j) % 4).wait_send()
    for j in range(1, heads):
        target = (mine + j) % heads
        query_to(target).wait_send()
        for copy in cache_out(target) + part_to(target):
            copy.wait_send()
    for source in range(heads):
        for j in range(1, spread_count):
            for copy in cache_on(source, j, False):
                copy.wait_send()


def on_device(
    states_in,
    w_qkv,
    qk_gain,
    w_out,
    post_gain,
    w_gate_up,
    w_down,
    cache_keys,
    cache_values,
    slot_node,
    node_length,
    node_parent,
    leaf_segment,
    leaf_node,
):
    rows, width = states_in.shape
    here = w_qkv.shape[2]
    heads = here // HD
    node_rows = cache_keys.shape[1]
    own_rows = rows // 4
    units = w_down.shape[0]
    slots = slot_node.shape[0]
    spread_count = slots // heads
    lines = slots // 2
    tiles = 4
    vmem = pl.BlockSpec(memory_space=pltpu.VMEM)
    smem = pl.BlockSpec(memory_space=pltpu.SMEM)
    hbm = pl.BlockSpec(memory_space=pl.ANY)
    dma = pltpu.SemaphoreType.DMA
    half = HD // 2
    frequency = THETA ** (-2.0 * jnp.arange(half, dtype=F32) / HD)

    def per_head(kind):
        return pltpu.VMEM((heads, rows, HD), kind)

    cached = pltpu.VMEM((spread_count, heads * node_rows, HD), BF16)
    part = pltpu.VMEM((lines, own_rows, width), BF16)
    return pl.pallas_call(
        functools.partial(layer_kernel, spread_count),
        out_shape=jax.ShapeDtypeStruct((own_rows, width), BF16),
        in_specs=[vmem, hbm, vmem, hbm, vmem, hbm, hbm, hbm, hbm, smem, smem, smem, vmem, smem, vmem],
        out_specs=vmem,
        scratch_shapes=[
            pltpu.VMEM(w_qkv.shape, BF16),
            pltpu.VMEM(w_out.shape, BF16),
            pltpu.VMEM((3, rows, here), F32),
            per_head(BF16),
            per_head(BF16),
            pltpu.VMEM((rows, here), BF16),
            pltpu.VMEM((4, 8, rows), F32),
            per_head(BF16),
            cached,
            cached,
            pltpu.VMEM((rows, HD), F32),
            pltpu.VMEM((rows, HD), F32),
            per_head(F32),
            pltpu.VMEM((rows, HD), F32),
            per_head(F32), per_head(F32), per_head(F32),
            per_head(F32), per_head(F32), per_head(F32),
            per_head(BF16), per_head(BF16),
            pltpu.VMEM((heads, 8, rows), F32),
            pltpu.VMEM((heads, 8, rows), F32),
            pltpu.VMEM((rows, here), BF16),
            pltpu.VMEM((rows, width), F32),
            pltpu.VMEM((rows, width), BF16),
            pltpu.VMEM((2, own_rows, width), BF16),
            pltpu.VMEM((own_rows, width), BF16),
            pltpu.VMEM((own_rows, width), BF16),
            pltpu.VMEM((own_rows, width), BF16),
            pltpu.VMEM((slots * own_rows, width), BF16),
            pltpu.VMEM(w_gate_up.shape, BF16),
            pltpu.VMEM(w_down.shape, BF16),
            pltpu.VMEM((2 * own_rows, units), BF16),
            pltpu.VMEM((2 * own_rows, width), F32),
            pltpu.VMEM((2, own_rows, width), F32),
            pltpu.VMEM((own_rows, width), F32),
            part, part, part,
            dma((7,)),
            dma((4,)), dma((4,)),
            dma((heads,)), dma((heads,)),
            dma((2,)),
            dma((spread_count, heads)), dma((heads, spread_count)),
            dma((spread_count, heads)), dma((heads, spread_count)),
            dma((heads,)), dma((heads,)),
            dma((heads,)), dma((heads,)),
            dma((2, tiles)), dma((2, tiles)),
            dma((tiles,)), dma((tiles,)),
            dma((3, slots)),
            dma((slots,)),
            dma((lines, tiles)), dma((lines, tiles)),
            dma((lines, tiles)), dma((lines, tiles)),
        ],
        compiler_params=pltpu.CompilerParams(
            collective_id=1, has_side_effects=True, vmem_limit_bytes=62 * 2**20
        ),
    )(
        states_in, w_qkv, qk_gain, w_out, post_gain, w_gate_up, w_down, cache_keys, cache_values,
        slot_node, node_length, node_parent, leaf_segment, leaf_node,
        jnp.concatenate([frequency, frequency])[None, :],
    )


def solution(mesh):
    placed = (
        P("blk", None),
        P(None, None, "head"),
        P(None, "head"),
        P("head", None),
        P(),
        P(None, None, "blk"),
        P("blk", None),
        P("blk", None, "head"),
        P("blk", None, "head"),
        P(),
        P(),
        P(),
        P(),
        P(),
    )
    return jax.shard_map(
        on_device, mesh=mesh, in_specs=placed, out_specs=P(("blk", "head"), None), check_vma=False
    )
```

```python
import functools

import jax
import jax.numpy as jnp
from jax import lax
from jax.experimental import pallas as pl
from jax.experimental.pallas import tpu as pltpu
from jax.sharding import PartitionSpec as P

HD = 128
EPS = 1e-06
THETA = 500000.0
NEG = -1e30
MESH = pl.DeviceIdType.MESH
BF16 = jnp.bfloat16
F32 = jnp.float32


def by_distance(at, count, step):
    back = count - 1 - at
    near = jnp.minimum(at, back)
    both = jnp.where(step % 2 == 1, at - (step + 1) // 2, at + step // 2)
    return jnp.where(step <= 2 * near, both, jnp.where(at < back, step, count - 1 - step))


def remote(src, dst, send_sem, recv_sem, **where):
    return pltpu.make_async_remote_copy(
        src_ref=src,
        dst_ref=dst,
        send_sem=send_sem,
        recv_sem=recv_sem,
        device_id=where,
        device_id_type=MESH,
    )


def meet(peers):
    barrier = pltpu.get_barrier_semaphore()
    for peer in peers:
        pl.semaphore_signal(barrier, inc=1, device_id=peer, device_id_type=MESH)
    return lambda: pl.semaphore_wait(barrier, len(peers))


def mlp_part(
    lines, loads,
    mid_ref, gain_ref, out_ref,
    gathered, wgu, wd, hidden, whole, own_part, own_sum, send_x, recv_x, recv_z,
    g_send, g_recv, x_send, x_recv, z_send, z_recv,
):
    rows, width = mid_ref.shape
    units = wd.shape[0]
    me = lax.axis_index("blk")
    z, x = me // 2, me % 2
    other = z * 2 + 1 - x

    def block(index):
        return gathered.at[pl.ds(pl.multiple_of(index * rows, rows), rows)]

    def pass_on(index, way, target):
        return remote(block(index), block(index), g_send.at[way, index], g_recv.at[index], blk=target)

    def spread(origin, wait):
        index = origin * 2 + x
        if wait:
            pass_on(index, 0, other).wait_recv()

        @pl.when((origin - z) * (origin - z) != 1)
        def _():
            pass_on(index, 0, other).start()

        @pl.when((origin <= z) & (z < lines - 1))
        def _():
            pass_on(index, 1, me + 2).start()

        @pl.when((origin >= z) & (z > 0))
        def _():
            pass_on(index, 2, me - 2).start()

    gathered[pl.ds(pl.multiple_of(me * rows, rows), rows), :] = mid_ref[...]
    spread(z, False)

    tiles = x_send.shape[1]
    wide = width // tiles

    def cols_of(t):
        return pl.ds(pl.multiple_of(t * wide, wide), wide)

    def to_x(origin, t):
        return remote(
            send_x.at[origin, :, cols_of(t)], recv_x.at[origin, :, cols_of(t)],
            x_send.at[origin, t], x_recv.at[origin, t], blk=other,
        )

    def to_z(origin, t):
        return remote(
            send_x.at[origin, :, cols_of(t)], recv_z.at[z, :, cols_of(t)],
            z_send.at[origin, t], z_recv.at[z, t], blk=origin * 2 + x,
        )

    def reduce_x(step):
        origin = by_distance(z, lines, step)

        @pl.loop(0, tiles)
        def _(t):
            at = cols_of(t)
            to_x(origin, t).wait_recv()
            summed = own_part[step % 2, :, at] + recv_x[origin, :, at].astype(F32)
            to_x(origin, t).wait_send()
            send_x[origin, :, at] = summed.astype(BF16)
            to_z(origin, t).start()
            if step == lines - 1:
                to_x(z, t).start()

    tile = min(256, units)
    for step in range(lines):
        origin = by_distance(z, lines, step)
        if step + 1 < lines:
            spread(by_distance(z, lines, step + 1), True)
        pass_on(origin * 2 + 1 - x, 0, other).wait_recv()
        if step == 0:
            @pl.when(z < lines - 1)
            def _():
                pass_on(other, 1, me + 2).start()

            @pl.when(z > 0)
            def _():
                pass_on(other, 2, me - 2).start()

            loads[0].wait()
            loads[1].wait()
        chunk = pl.ds(pl.multiple_of(origin * 2 * rows, 2 * rows), 2 * rows)

        @pl.loop(0, units // tile)
        def _(t):
            at = pl.ds(pl.multiple_of(t * tile, tile), tile)
            state = gathered[chunk, :]
            gate = jnp.dot(state, wgu[0, :, at], preferred_element_type=F32)
            up = jnp.dot(state, wgu[1, :, at], preferred_element_type=F32)
            hidden[:, at] = (gate / (1.0 + jnp.exp(-gate)) * up).astype(BF16)

        if step == 0:
            loads[2].wait()

        @pl.loop(0, tiles)
        def _(t):
            at = cols_of(t)
            whole[:, at] = jnp.dot(hidden[...], wd[:, at], preferred_element_type=F32)
            kept = whole[pl.ds(pl.multiple_of(x * rows, rows), rows), at]
            if step == 0:
                own_sum[:, at] = kept
            else:
                own_part[step % 2, :, at] = kept
            send_x[origin, :, at] = whole[
                pl.ds(pl.multiple_of((1 - x) * rows, rows), rows), at
            ].astype(BF16)
            if step > 0:
                to_x(origin, t).start()

        if step > 1:
            reduce_x(step - 1)
    reduce_x(lines - 1)

    for t in range(tiles):
        to_x(z, t).wait_recv()
    total = own_sum[...] + recv_x[z].astype(F32)
    for j in range(1, lines):
        source = (z + j) % lines
        for t in range(tiles):
            spot = recv_z.at[source, :, cols_of(t)]
            remote(spot, spot, z_send.at[0, t], z_recv.at[source, t], blk=other).wait_recv()
        total = total + recv_z[source].astype(F32)
    scale = lax.rsqrt(jnp.mean(total * total, axis=-1, keepdims=True) + EPS)
    out_ref[...] = (mid_ref[...].astype(F32) + total * scale * gain_ref[1:2, :]).astype(BF16)

    for t in range(tiles):
        to_x(z, t).wait_send()

    @pl.when(z < lines - 1)
    def _():
        pass_on(other, 1, me + 2).wait_send()

    @pl.when(z > 0)
    def _():
        pass_on(other, 2, me - 2).wait_send()

    for origin in range(lines):
        index = origin * 2 + x

        @pl.when((origin - z) * (origin - z) != 1)
        def _():
            pass_on(index, 0, other).wait_send()

        @pl.when((origin <= z) & (z < lines - 1))
        def _():
            pass_on(index, 1, me + 2).wait_send()

        @pl.when((origin >= z) & (z > 0))
        def _():
            pass_on(index, 2, me - 2).wait_send()

        @pl.when(origin != z)
        def _():
            for t in range(tiles):
                to_z(origin, t).wait_send()


def layer_kernel(
    spread_count,
    states_ref, wqkv_hbm, gain_ref, wout_hbm, post_ref, wgu_hbm, wd_hbm, keys_hbm, values_hbm,
    slot_node, node_length, node_parent, segment_ref, leaf_node, frequency_ref, out_ref,
    wqkv, wout, raw, query, key, value, squares, query_in, keys_in, values_in,
    cos_ref, sin_ref, limits, own_info,
    peak, norm, acc, leaf_peak, leaf_norm, leaf_acc, part_out, part_in, stat_out, stat_in,
    attended, proj, proj_low, pair_in, pair_out, line_in, mid_ref,
    gathered, wgu, wd, hidden, whole, own_part, own_sum, send_x, recv_x, recv_z,
    w_sem, s_send, s_recv, q_send, q_recv, own_sem, k_send, k_recv, v_send, v_recv,
    p_send, p_recv, t_send, t_recv, c_send, c_recv, y_send, y_recv,
    g_send, g_recv, x_send, x_recv, z_send, z_recv,
):
    rows, width = states_ref.shape
    heads = query.shape[0]
    node_rows = keys_hbm.shape[1]
    slots = slot_node.shape[0]
    me = lax.axis_index("blk")
    head = lax.axis_index("head")
    mine, rest = me // spread_count, me % spread_count
    scale = HD ** (-0.5)

    loads = [pltpu.make_async_copy(wqkv_hbm.at[c], wqkv.at[c], w_sem.at[c]) for c in range(3)]
    loads.append(pltpu.make_async_copy(wout_hbm, wout, w_sem.at[3]))
    late = [
        pltpu.make_async_copy(wgu_hbm.at[0], wgu.at[0], w_sem.at[4]),
        pltpu.make_async_copy(wgu_hbm.at[1], wgu.at[1], w_sem.at[5]),
        pltpu.make_async_copy(wd_hbm, wd, w_sem.at[6]),
    ]
    for load in loads:
        load.start()

    def holder(index):
        return index * spread_count + rest

    peers = [{"head": (head + j) % 4} for j in range(1, 4)]
    peers += [{"blk": holder((mine + j) % heads)} for j in range(1, heads)]
    peers += [{"blk": mine * spread_count + (rest + j) % spread_count} for j in range(1, spread_count)]
    lines = slots // 2
    if spread_count != 2:
        peers += [{"blk": me // 2 * 2 + 1 - me % 2}]
        peers += [{"blk": (me // 2 + j) % lines * 2 + me % 2} for j in range(1, lines)]
    all_here = meet(peers)

    def column(index):
        return pl.ds(pl.multiple_of(index * HD, HD), HD)

    def place(buffer, index, member):
        return buffer.at[member, pl.ds(pl.multiple_of(index * node_rows, node_rows), node_rows)]

    def cache_out(target):
        return (
            remote(keys_hbm.at[0, :, column(target)], place(keys_in, mine, rest), k_send.at[0, target], k_recv.at[mine, rest], blk=holder(target)),
            remote(values_hbm.at[0, :, column(target)], place(values_in, mine, rest), v_send.at[0, target], v_recv.at[mine, rest], blk=holder(target)),
        )

    def cache_wait(source, member):
        far = holder((mine + 1) % heads)
        spot, spot_too = place(keys_in, source, member), place(values_in, source, member)
        remote(spot, spot, k_send.at[0, 0], k_recv.at[source, member], blk=far).wait_recv()
        remote(spot_too, spot_too, v_send.at[0, 0], v_recv.at[source, member], blk=far).wait_recv()

    def cache_on(source, j, own):
        target = mine * spread_count + (rest + j) % spread_count
        spot, spot_too = place(keys_in, source, rest), place(values_in, source, rest)
        from_keys = keys_hbm.at[0, :, column(mine)] if own else spot
        from_values = values_hbm.at[0, :, column(mine)] if own else spot_too
        return (
            remote(from_keys, spot, k_send.at[j, source], k_recv.at[source, rest], blk=target),
            remote(from_values, spot_too, v_send.at[j, source], v_recv.at[source, rest], blk=target),
        )

    own_copies = [
        pltpu.make_async_copy(keys_hbm.at[0, :, column(mine)], place(keys_in, mine, rest), own_sem.at[0]),
        pltpu.make_async_copy(values_hbm.at[0, :, column(mine)], place(values_in, mine, rest), own_sem.at[1]),
    ]
    for copy in own_copies:
        copy.start()

    def pass_on(step):
        source = by_distance(mine, heads, step)
        cache_wait(source, rest)
        for j in range(1, spread_count):
            for copy in cache_on(source, j, False):
                copy.start()

    leaves, middles, nodes = leaf_node.shape[1], node_parent.shape[0], node_length.shape[0]

    def upright(lines_of):
        filled = HD - len(lines_of)
        return jnp.transpose(jnp.concatenate(lines_of + [jnp.zeros((filled, rows), F32)], axis=0))

    def seen_by(group):
        segment = segment_ref[pl.ds(group, 1), :]
        middle, root = jnp.zeros_like(segment), jnp.zeros_like(segment)
        for leaf in range(leaves):
            middle = jnp.where(segment == leaf, leaf_node[group, leaf], middle)
        for index in range(middles):
            root = jnp.where(middle == nodes - middles + index, node_parent[index], root)
        middle_rows, root_rows = jnp.zeros_like(segment), jnp.zeros_like(segment)
        for node in range(nodes):
            middle_rows = jnp.where(middle == node, node_length[node], middle_rows)
            root_rows = jnp.where(root == node, node_length[node], root_rows)
        return segment, middle, root, middle_rows, root_rows

    for g in range(heads):
        _, middle, root, middle_rows, root_rows = seen_by(holder(g))
        lines_of = []
        for j in range(spread_count):
            for index in range(heads):
                node = slot_node[index * spread_count + (rest + j) % spread_count]
                row = jnp.where(middle == node, middle_rows, jnp.where(root == node, root_rows, 0))
                lines_of.append(row.astype(F32))
        limits[g] = upright(lines_of)
    segment, _, _, middle_rows, root_rows = seen_by(me)
    first = jnp.zeros(segment.shape, F32)
    start = jnp.zeros((1, 1), F32)
    for leaf in range(leaves):
        inside = (segment == leaf).astype(F32)
        first = first + inside * start
        start = start + jnp.sum(inside, axis=-1, keepdims=True)
    token = lax.broadcasted_iota(jnp.int32, (1, rows), 1)
    position = (middle_rows + root_rows + token).astype(F32) - first
    own_info[...] = upright([first, position])

    all_here()
    for j in range(1, heads):
        for copy in cache_out((mine + j) % heads):
            copy.start()
    for j in range(1, spread_count):
        for copy in cache_on(mine, j, True):
            copy.start()

    tile = 2 * HD
    here = heads * HD

    def product(c):
        loads[c].wait()

        @pl.loop(0, here // tile)
        def _(t):
            at = pl.ds(pl.multiple_of(t * tile, tile), tile)
            raw[c, :, at] = jnp.dot(states_ref[...], wqkv[c, :, at], preferred_element_type=F32)

    lane = lax.broadcasted_iota(jnp.int32, (rows, HD), 1)
    product(0)
    product(1)
    query_sum = jnp.sum(raw[0] * raw[0], axis=-1, keepdims=True)
    key_sum = jnp.sum(raw[1] * raw[1], axis=-1, keepdims=True)
    packed = jnp.where(lane == 0, query_sum, jnp.where(lane == 1, key_sum, 0.0))
    squares[head] = jnp.transpose(packed)[0:8]

    def squares_to(target):
        return remote(squares.at[head], squares.at[head], s_send.at[target], s_recv.at[head], head=target)

    for j in range(1, 4):
        squares_to((head + j) % 4).start()
    product(2)
    for load in late:
        load.start()
    value[...] = raw[2].astype(BF16)
    angles = own_info[:, 1:2] * frequency_ref[...]
    cos_ref[...] = jnp.cos(angles)
    sines = jnp.sin(angles)
    sin_ref[...] = jnp.where(lane < HD // 2, -sines, sines)
    total = squares[head]
    for j in range(1, 4):
        source = (head + j) % 4
        remote(squares.at[source], squares.at[source], s_send.at[source], s_recv.at[source], head=source).wait_recv()
        total = total + squares[source]
    spread = jnp.transpose(jnp.concatenate([total] * (HD // 8), axis=0))
    scales = lax.rsqrt(spread / width + EPS)
    query_scale, key_scale = scales[:, 0:1], scales[:, 1:2]

    def turned(c, h, by):
        at = slice(h * HD, (h + 1) * HD)
        normed = raw[c, :, at] * by * gain_ref[c : c + 1, at]
        swapped = pltpu.roll(normed, HD // 2, 1)
        return (normed * cos_ref[...] + swapped * sin_ref[...]).astype(BF16)

    for h in range(heads):
        query[h] = turned(0, h, query_scale)

    def query_to(target):
        return remote(query.at[target], query_in.at[mine], q_send.at[target], q_recv.at[mine], blk=holder(target))

    for j in range(1, heads):
        query_to((mine + j) % heads).start()
    query_in[mine] = query[mine]
    for step in range(1, heads):
        pass_on(step)
    for h in range(heads):
        key[h] = turned(1, h, key_scale)

    row_at = lax.broadcasted_iota(jnp.int32, (rows, rows), 0)
    key_at = lax.broadcasted_iota(jnp.int32, (rows, rows), 1)
    see_leaf = (key_at.astype(F32) >= own_info[:, 0:1]) & (key_at <= row_at)
    over = (((1,), (1,)), ((), ()))
    for h in range(heads):
        scores = lax.dot_general(query[h], key[h], over, preferred_element_type=F32) * scale
        scores = jnp.where(see_leaf, scores, NEG)
        top = jnp.max(scores, axis=-1, keepdims=True)
        weights = jnp.exp(scores - top)
        leaf_peak[h] = jnp.broadcast_to(top, (rows, HD))
        leaf_norm[h] = jnp.broadcast_to(jnp.sum(weights, axis=-1, keepdims=True), (rows, HD))
        leaf_acc[h] = jnp.dot(weights.astype(BF16), value[:, h * HD : (h + 1) * HD], preferred_element_type=F32)

    for j in range(1, heads):
        source = (mine + j) % heads
        remote(query.at[0], query_in.at[source], q_send.at[0], q_recv.at[source], blk=holder(source)).wait_recv()
    key_row = lax.broadcasted_iota(jnp.int32, (rows, node_rows), 1).astype(F32)

    def part_to(target):
        return (
            remote(part_out.at[target], part_in.at[mine], p_send.at[target], p_recv.at[mine], blk=holder(target)),
            remote(stat_out.at[target], stat_in.at[mine], t_send.at[target], t_recv.at[mine], blk=holder(target)),
        )

    for copy in own_copies:
        copy.wait()
    for j in range(spread_count):
        member = (rest + j) % spread_count
        if j > 0:
            for step in range(heads):
                cache_wait(by_distance(mine, heads, step), member)

        @pl.loop(0, heads)
        def _(turn):
            g = (mine + 1 + turn) % heads
            scores = lax.dot_general(query_in[g], keys_in[member], over, preferred_element_type=F32) * scale
            limit = limits[g]
            masked = [
                jnp.where(
                    key_row < limit[:, j * heads + index : j * heads + index + 1],
                    scores[:, index * node_rows : (index + 1) * node_rows],
                    NEG,
                )
                for index in range(heads)
            ]
            highest = functools.reduce(jnp.maximum, masked)
            top = jnp.max(highest, axis=-1, keepdims=True)
            if j > 0:
                top = jnp.maximum(top, peak[g][:, 0:1])
            weights = [jnp.exp(part - top) for part in masked]
            total = jnp.sum(functools.reduce(jnp.add, weights), axis=-1, keepdims=True)
            summed = jnp.dot(
                jnp.concatenate([part.astype(BF16) for part in weights], axis=-1),
                values_in[member],
                preferred_element_type=F32,
            )
            if j > 0:
                shrink = jnp.exp(peak[g][:, 0:1] - top)
                total = total + norm[g][:, 0:1] * shrink
                summed = summed + acc[g] * shrink
            if j < spread_count - 1:
                peak[g] = jnp.broadcast_to(top, (rows, HD))
                norm[g] = jnp.broadcast_to(total, (rows, HD))
                acc[g] = summed
            else:
                part_out[g] = (summed / total).astype(BF16)
                stats = jnp.where(lane == 0, top, jnp.where(lane == 1, total, 0.0))
                stat_out[g] = jnp.transpose(stats)[0:8]

                @pl.when(turn < heads - 1)
                def _():
                    for copy in part_to(g):
                        copy.start()

    part_in[mine] = part_out[mine]
    stat_in[mine] = stat_out[mine]
    for j in range(1, heads):
        source = (mine + j) % heads
        remote(part_out.at[0], part_in.at[source], p_send.at[0], p_recv.at[source], blk=holder(source)).wait_recv()
        remote(stat_out.at[0], stat_in.at[source], t_send.at[0], t_recv.at[source], blk=holder(source)).wait_recv()
    for h in range(heads):
        stats = jnp.transpose(jnp.concatenate([stat_in[h]] * (HD // 8), axis=0))
        other_peak, other_norm = stats[:, 0:1], stats[:, 1:2]
        top = jnp.maximum(leaf_peak[h], other_peak)
        own_scale = jnp.exp(leaf_peak[h] - top)
        other_scale = jnp.exp(other_peak - top) * other_norm
        summed = leaf_acc[h] * own_scale + part_in[h].astype(F32) * other_scale
        attended[:, h * HD : (h + 1) * HD] = (
            summed / (leaf_norm[h] * own_scale + other_scale)
        ).astype(BF16)

    loads[3].wait()
    y, core = head // 2, head % 2
    own_rows = out_ref.shape[0]
    sibling, across = y * 2 + 1 - core, (1 - y) * 2 + core
    tiles = c_send.shape[1]
    wide = width // tiles

    def rows_of(index):
        return pl.ds(pl.multiple_of(index * own_rows, own_rows), own_rows)

    def cols_of(t):
        return pl.ds(t * wide, wide)

    def to_pair(half, t):
        return remote(
            proj_low.at[rows_of(half * 2 + 1 - core), cols_of(t)],
            pair_in.at[half, :, cols_of(t)],
            c_send.at[half, t], c_recv.at[half, t], head=sibling,
        )

    def to_line(t):
        return remote(pair_out.at[:, cols_of(t)], line_in.at[:, cols_of(t)], y_send.at[t], y_recv.at[t], head=across)

    def on_line(t):
        to_pair(1 - y, t).wait_recv()
        pair_out[:, cols_of(t)] = (
            proj[rows_of(across), cols_of(t)] + pair_in[1 - y, :, cols_of(t)].astype(F32)
        ).astype(BF16)
        to_line(t).start()

    for t in range(tiles):
        tiled = jnp.dot(attended[...], wout[:, cols_of(t)], preferred_element_type=F32)
        proj[:, cols_of(t)] = tiled
        proj_low[:, cols_of(t)] = tiled.astype(BF16)
        to_pair(1 - y, t).start()
        to_pair(y, t).start()
        if t > 0:
            on_line(t - 1)
    on_line(tiles - 1)
    for t in range(tiles):
        to_pair(y, t).wait_recv()
        to_line(t).wait_recv()
    total = proj[rows_of(head), :] + pair_in[y].astype(F32) + line_in[...].astype(F32)
    shrink = lax.rsqrt(jnp.mean(total * total, axis=-1, keepdims=True) + EPS)
    own = states_ref[rows_of(head), :].astype(F32)
    mid_ref[...] = (own + total * shrink * post_ref[0:1, :]).astype(BF16)

    mlp_part(
        lines, late,
        mid_ref, post_ref, out_ref,
        gathered, wgu, wd, hidden, whole, own_part, own_sum, send_x, recv_x, recv_z,
        g_send, g_recv, x_send, x_recv, z_send, z_recv,
    )

    for t in range(tiles):
        to_line(t).wait_send()
        for half in range(2):
            to_pair(half, t).wait_send()
    for j in range(1, 4):
        squares_to((head + j) % 4).wait_send()
    for j in range(1, heads):
        target = (mine + j) % heads
        query_to(target).wait_send()
        for copy in cache_out(target) + part_to(target):
            copy.wait_send()
    for source in range(heads):
        for j in range(1, spread_count):
            for copy in cache_on(source, j, False):
                copy.wait_send()


def on_device(
    states_in,
    w_qkv,
    qk_gain,
    w_out,
    post_gain,
    w_gate_up,
    w_down,
    cache_keys,
    cache_values,
    slot_node,
    node_length,
    node_parent,
    leaf_segment,
    leaf_node,
):
    rows, width = states_in.shape
    here = w_qkv.shape[2]
    heads = here // HD
    node_rows = cache_keys.shape[1]
    own_rows = rows // 4
    units = w_down.shape[0]
    slots = slot_node.shape[0]
    spread_count = slots // heads
    lines = slots // 2
    tiles = 4
    vmem = pl.BlockSpec(memory_space=pltpu.VMEM)
    smem = pl.BlockSpec(memory_space=pltpu.SMEM)
    hbm = pl.BlockSpec(memory_space=pl.ANY)
    dma = pltpu.SemaphoreType.DMA
    half = HD // 2
    frequency = THETA ** (-2.0 * jnp.arange(half, dtype=F32) / HD)

    def per_head(kind):
        return pltpu.VMEM((heads, rows, HD), kind)

    cached = pltpu.VMEM((spread_count, heads * node_rows, HD), BF16)
    part = pltpu.VMEM((lines, own_rows, width), BF16)
    return pl.pallas_call(
        functools.partial(layer_kernel, spread_count),
        out_shape=jax.ShapeDtypeStruct((own_rows, width), BF16),
        in_specs=[vmem, hbm, vmem, hbm, vmem, hbm, hbm, hbm, hbm, smem, smem, smem, vmem, smem, vmem],
        out_specs=vmem,
        scratch_shapes=[
            pltpu.VMEM(w_qkv.shape, BF16),
            pltpu.VMEM(w_out.shape, BF16),
            pltpu.VMEM((3, rows, here), F32),
            per_head(BF16),
            per_head(BF16),
            pltpu.VMEM((rows, here), BF16),
            pltpu.VMEM((4, 8, rows), F32),
            per_head(BF16),
            cached,
            cached,
            pltpu.VMEM((rows, HD), F32),
            pltpu.VMEM((rows, HD), F32),
            per_head(F32),
            pltpu.VMEM((rows, HD), F32),
            per_head(F32), per_head(F32), per_head(F32),
            per_head(F32), per_head(F32), per_head(F32),
            per_head(BF16), per_head(BF16),
            pltpu.VMEM((heads, 8, rows), F32),
            pltpu.VMEM((heads, 8, rows), F32),
            pltpu.VMEM((rows, here), BF16),
            pltpu.VMEM((rows, width), F32),
            pltpu.VMEM((rows, width), BF16),
            pltpu.VMEM((2, own_rows, width), BF16),
            pltpu.VMEM((own_rows, width), BF16),
            pltpu.VMEM((own_rows, width), BF16),
            pltpu.VMEM((own_rows, width), BF16),
            pltpu.VMEM((slots * own_rows, width), BF16),
            pltpu.VMEM(w_gate_up.shape, BF16),
            pltpu.VMEM(w_down.shape, BF16),
            pltpu.VMEM((2 * own_rows, units), BF16),
            pltpu.VMEM((2 * own_rows, width), F32),
            pltpu.VMEM((2, own_rows, width), F32),
            pltpu.VMEM((own_rows, width), F32),
            part, part, part,
            dma((7,)),
            dma((4,)), dma((4,)),
            dma((heads,)), dma((heads,)),
            dma((2,)),
            dma((spread_count, heads)), dma((heads, spread_count)),
            dma((spread_count, heads)), dma((heads, spread_count)),
            dma((heads,)), dma((heads,)),
            dma((heads,)), dma((heads,)),
            dma((2, tiles)), dma((2, tiles)),
            dma((tiles,)), dma((tiles,)),
            dma((3, slots)),
            dma((slots,)),
            dma((lines, tiles)), dma((lines, tiles)),
            dma((lines, tiles)), dma((lines, tiles)),
        ],
        compiler_params=pltpu.CompilerParams(
            collective_id=1, has_side_effects=True, vmem_limit_bytes=62 * 2**20
        ),
    )(
        states_in, w_qkv, qk_gain, w_out, post_gain, w_gate_up, w_down, cache_keys, cache_values,
        slot_node, node_length, node_parent, leaf_segment, leaf_node,
        jnp.concatenate([frequency, frequency])[None, :],
    )


def solution(mesh):
    placed = (
        P("blk", None),
        P(None, None, "head"),
        P(None, "head"),
        P("head", None),
        P(),
        P(None, None, "blk"),
        P("blk", None),
        P("blk", None, "head"),
        P("blk", None, "head"),
        P(),
        P(),
        P(),
        P(),
        P(),
    )
    return jax.shard_map(
        on_device, mesh=mesh, in_specs=placed, out_specs=P(("blk", "head"), None), check_vma=False
    )
```

```python
import functools

import jax
import jax.numpy as jnp
import numpy as np
from jax import lax
from jax.experimental import pallas as pl
from jax.experimental.pallas import tpu as pltpu
from jax.sharding import PartitionSpec as P

HD = 128
EPS = 1e-06
THETA = 500000.0
NEG = -1e30
MESH = pl.DeviceIdType.MESH
BF16 = jnp.bfloat16
F32 = jnp.float32


def by_distance(at, count, step):
    back = count - 1 - at
    near = jnp.minimum(at, back)
    both = jnp.where(step % 2 == 1, at - (step + 1) // 2, at + step // 2)
    return jnp.where(step <= 2 * near, both, jnp.where(at < back, step, count - 1 - step))


def remote(src, dst, send_sem, recv_sem, **where):
    return pltpu.make_async_remote_copy(
        src_ref=src,
        dst_ref=dst,
        send_sem=send_sem,
        recv_sem=recv_sem,
        device_id=where,
        device_id_type=MESH,
    )


def meet(peers):
    barrier = pltpu.get_barrier_semaphore()
    for peer in peers:
        pl.semaphore_signal(barrier, inc=1, device_id=peer, device_id_type=MESH)
    return lambda: pl.semaphore_wait(barrier, len(peers))


def mlp_part(
    lines, loads,
    mid_ref, gain_ref, out_ref,
    gathered, wgu, wd, hidden, whole, own_part, own_sum, send_x, recv_x, recv_z,
    g_send, g_recv, x_send, x_recv, z_send, z_recv,
):
    rows, width = mid_ref.shape
    units = wd.shape[0]
    me = lax.axis_index("blk")
    z, x = me // 2, me % 2
    other = z * 2 + 1 - x

    def block(index):
        return gathered.at[pl.ds(pl.multiple_of(index * rows, rows), rows)]

    def pass_on(index, way, target):
        return remote(block(index), block(index), g_send.at[way, index], g_recv.at[index], blk=target)

    def spread(origin, wait):
        index = origin * 2 + x
        if wait:
            pass_on(index, 0, other).wait_recv()

        @pl.when((origin - z) * (origin - z) != 1)
        def _():
            pass_on(index, 0, other).start()

        @pl.when((origin <= z) & (z < lines - 1))
        def _():
            pass_on(index, 1, me + 2).start()

        @pl.when((origin >= z) & (z > 0))
        def _():
            pass_on(index, 2, me - 2).start()

    gathered[pl.ds(pl.multiple_of(me * rows, rows), rows), :] = mid_ref[...]
    spread(z, False)

    tiles = x_send.shape[1]
    wide = width // tiles

    def cols_of(t):
        return pl.ds(pl.multiple_of(t * wide, wide), wide)

    def to_x(origin, t):
        return remote(
            send_x.at[origin, :, cols_of(t)], recv_x.at[origin, :, cols_of(t)],
            x_send.at[origin, t], x_recv.at[origin, t], blk=other,
        )

    def to_z(origin, t):
        return remote(
            send_x.at[origin, :, cols_of(t)], recv_z.at[z, :, cols_of(t)],
            z_send.at[origin, t], z_recv.at[z, t], blk=origin * 2 + x,
        )

    def reduce_x(step):
        origin = by_distance(z, lines, step)

        @pl.loop(0, tiles)
        def _(t):
            at = cols_of(t)
            to_x(origin, t).wait_recv()
            summed = own_part[step % 2, :, at] + recv_x[origin, :, at].astype(F32)
            to_x(origin, t).wait_send()
            send_x[origin, :, at] = summed.astype(BF16)
            to_z(origin, t).start()
            if step == lines - 1:
                to_x(z, t).start()

    tile = min(256, units)
    for step in range(lines):
        origin = by_distance(z, lines, step)
        if step + 1 < lines:
            spread(by_distance(z, lines, step + 1), True)
        pass_on(origin * 2 + 1 - x, 0, other).wait_recv()
        if step == 0:
            @pl.when(z < lines - 1)
            def _():
                pass_on(other, 1, me + 2).start()

            @pl.when(z > 0)
            def _():
                pass_on(other, 2, me - 2).start()

            loads[0].wait()
            loads[1].wait()
        chunk = pl.ds(pl.multiple_of(origin * 2 * rows, 2 * rows), 2 * rows)

        @pl.loop(0, units // tile)
        def _(t):
            at = pl.ds(pl.multiple_of(t * tile, tile), tile)
            state = gathered[chunk, :]
            gate = jnp.dot(state, wgu[0, :, at], preferred_element_type=F32)
            up = jnp.dot(state, wgu[1, :, at], preferred_element_type=F32)
            hidden[:, at] = (gate / (1.0 + jnp.exp(-gate)) * up).astype(BF16)

        if step == 0:
            loads[2].wait()

        @pl.loop(0, tiles)
        def _(t):
            at = cols_of(t)
            whole[:, at] = jnp.dot(hidden[...], wd[:, at], preferred_element_type=F32)
            kept = whole[pl.ds(pl.multiple_of(x * rows, rows), rows), at]
            if step == 0:
                own_sum[:, at] = kept
            else:
                own_part[step % 2, :, at] = kept
            send_x[origin, :, at] = whole[
                pl.ds(pl.multiple_of((1 - x) * rows, rows), rows), at
            ].astype(BF16)
            if step > 0:
                to_x(origin, t).start()

        if step > 1:
            reduce_x(step - 1)
    reduce_x(lines - 1)

    for t in range(tiles):
        to_x(z, t).wait_recv()
    total = own_sum[...] + recv_x[z].astype(F32)
    for j in range(1, lines):
        source = (z + j) % lines
        for t in range(tiles):
            spot = recv_z.at[source, :, cols_of(t)]
            remote(spot, spot, z_send.at[0, t], z_recv.at[source, t], blk=other).wait_recv()
        total = total + recv_z[source].astype(F32)
    scale = lax.rsqrt(jnp.mean(total * total, axis=-1, keepdims=True) + EPS)
    out_ref[...] = (mid_ref[...].astype(F32) + total * scale * gain_ref[1:2, :]).astype(BF16)

    for t in range(tiles):
        to_x(z, t).wait_send()

    @pl.when(z < lines - 1)
    def _():
        pass_on(other, 1, me + 2).wait_send()

    @pl.when(z > 0)
    def _():
        pass_on(other, 2, me - 2).wait_send()

    for origin in range(lines):
        index = origin * 2 + x

        @pl.when((origin - z) * (origin - z) != 1)
        def _():
            pass_on(index, 0, other).wait_send()

        @pl.when((origin <= z) & (z < lines - 1))
        def _():
            pass_on(index, 1, me + 2).wait_send()

        @pl.when((origin >= z) & (z > 0))
        def _():
            pass_on(index, 2, me - 2).wait_send()

        @pl.when(origin != z)
        def _():
            for t in range(tiles):
                to_z(origin, t).wait_send()


def layer_kernel(
    spread_count,
    states_ref, wqkv_hbm, gain_ref, wout_hbm, post_ref, wgu_hbm, wd_hbm, keys_hbm, values_hbm,
    slot_node, node_length, node_parent, segment_ref, leaf_node, frequency_ref, out_ref,
    wqkv, wout, raw, query, key, value, squares, query_in, keys_in, values_in,
    cos_ref, sin_ref, limits, own_info,
    peak, norm, acc, leaf_peak, leaf_norm, leaf_acc, part_out, part_in, stat_out, stat_in,
    attended, proj, proj_low, pair_in, pair_out, line_in, mid_ref,
    gathered, wgu, wd, hidden, whole, own_part, own_sum, send_x, recv_x, recv_z,
    w_sem, s_send, s_recv, q_send, q_recv, own_sem, k_send, k_recv, v_send, v_recv,
    p_send, p_recv, t_send, t_recv, c_send, c_recv, y_send, y_recv,
    g_send, g_recv, x_send, x_recv, z_send, z_recv,
):
    rows, width = states_ref.shape
    heads = query.shape[0]
    node_rows = keys_hbm.shape[1]
    slots = slot_node.shape[0]
    me = lax.axis_index("blk")
    head = lax.axis_index("head")
    mine, rest = me // spread_count, me % spread_count
    scale = HD ** (-0.5)

    loads = [pltpu.make_async_copy(wqkv_hbm.at[c], wqkv.at[c], w_sem.at[c]) for c in range(3)]
    loads.append(pltpu.make_async_copy(wout_hbm, wout, w_sem.at[3]))
    late = [
        pltpu.make_async_copy(wgu_hbm.at[0], wgu.at[0], w_sem.at[4]),
        pltpu.make_async_copy(wgu_hbm.at[1], wgu.at[1], w_sem.at[5]),
        pltpu.make_async_copy(wd_hbm, wd, w_sem.at[6]),
    ]
    for load in loads:
        load.start()

    def holder(index):
        return index * spread_count + rest

    peers = [{"head": (head + j) % 4} for j in range(1, 4)]
    peers += [{"blk": holder((mine + j) % heads)} for j in range(1, heads)]
    peers += [{"blk": mine * spread_count + (rest + j) % spread_count} for j in range(1, spread_count)]
    lines = slots // 2
    if spread_count != 2:
        peers += [{"blk": me // 2 * 2 + 1 - me % 2}]
        peers += [{"blk": (me // 2 + j) % lines * 2 + me % 2} for j in range(1, lines)]
    all_here = meet(peers)

    def column(index):
        return pl.ds(pl.multiple_of(index * HD, HD), HD)

    def place(buffer, index, member):
        return buffer.at[member, pl.ds(pl.multiple_of(index * node_rows, node_rows), node_rows)]

    def cache_out(target):
        return (
            remote(keys_hbm.at[0, :, column(target)], place(keys_in, mine, rest), k_send.at[0, target], k_recv.at[mine, rest], blk=holder(target)),
            remote(values_hbm.at[0, :, column(target)], place(values_in, mine, rest), v_send.at[0, target], v_recv.at[mine, rest], blk=holder(target)),
        )

    def cache_wait(source, member):
        far = holder((mine + 1) % heads)
        spot, spot_too = place(keys_in, source, member), place(values_in, source, member)
        remote(spot, spot, k_send.at[0, 0], k_recv.at[source, member], blk=far).wait_recv()
        remote(spot_too, spot_too, v_send.at[0, 0], v_recv.at[source, member], blk=far).wait_recv()

    def cache_on(source, j, own):
        target = mine * spread_count + (rest + j) % spread_count
        spot, spot_too = place(keys_in, source, rest), place(values_in, source, rest)
        from_keys = keys_hbm.at[0, :, column(mine)] if own else spot
        from_values = values_hbm.at[0, :, column(mine)] if own else spot_too
        return (
            remote(from_keys, spot, k_send.at[j, source], k_recv.at[source, rest], blk=target),
            remote(from_values, spot_too, v_send.at[j, source], v_recv.at[source, rest], blk=target),
        )

    own_copies = [
        pltpu.make_async_copy(keys_hbm.at[0, :, column(mine)], place(keys_in, mine, rest), own_sem.at[0]),
        pltpu.make_async_copy(values_hbm.at[0, :, column(mine)], place(values_in, mine, rest), own_sem.at[1]),
    ]
    for copy in own_copies:
        copy.start()

    def pass_on(step):
        source = by_distance(mine, heads, step)
        cache_wait(source, rest)
        for j in range(1, spread_count):
            for copy in cache_on(source, j, False):
                copy.start()

    leaves, middles, nodes = leaf_node.shape[1], node_parent.shape[0], node_length.shape[0]

    def upright(lines_of):
        filled = HD - len(lines_of)
        return jnp.transpose(jnp.concatenate(lines_of + [jnp.zeros((filled, rows), F32)], axis=0))

    def seen_by(group):
        segment = segment_ref[pl.ds(group, 1), :]
        middle, root = jnp.zeros_like(segment), jnp.zeros_like(segment)
        for leaf in range(leaves):
            middle = jnp.where(segment == leaf, leaf_node[group, leaf], middle)
        for index in range(middles):
            root = jnp.where(middle == nodes - middles + index, node_parent[index], root)
        middle_rows, root_rows = jnp.zeros_like(segment), jnp.zeros_like(segment)
        for node in range(nodes):
            middle_rows = jnp.where(middle == node, node_length[node], middle_rows)
            root_rows = jnp.where(root == node, node_length[node], root_rows)
        return segment, middle, root, middle_rows, root_rows

    for g in range(heads):
        _, middle, root, middle_rows, root_rows = seen_by(holder(g))
        lines_of = []
        for j in range(spread_count):
            for index in range(heads):
                node = slot_node[index * spread_count + (rest + j) % spread_count]
                row = jnp.where(middle == node, middle_rows, jnp.where(root == node, root_rows, 0))
                lines_of.append(row.astype(F32))
        limits[g] = upright(lines_of)
    segment, _, _, middle_rows, root_rows = seen_by(me)
    first = jnp.zeros(segment.shape, F32)
    start = jnp.zeros((1, 1), F32)
    for leaf in range(leaves):
        inside = (segment == leaf).astype(F32)
        first = first + inside * start
        start = start + jnp.sum(inside, axis=-1, keepdims=True)
    token = lax.broadcasted_iota(jnp.int32, (1, rows), 1)
    position = (middle_rows + root_rows + token).astype(F32) - first
    own_info[...] = upright([first, position])

    all_here()
    for j in range(1, heads):
        for copy in cache_out((mine + j) % heads):
            copy.start()
    for j in range(1, spread_count):
        for copy in cache_on(mine, j, True):
            copy.start()

    tile = 2 * HD
    here = heads * HD

    def product(c):
        loads[c].wait()

        @pl.loop(0, here // tile)
        def _(t):
            at = pl.ds(pl.multiple_of(t * tile, tile), tile)
            raw[c, :, at] = jnp.dot(states_ref[...], wqkv[c, :, at], preferred_element_type=F32)

    lane = lax.broadcasted_iota(jnp.int32, (rows, HD), 1)
    product(0)
    product(1)
    query_sum = jnp.sum(raw[0] * raw[0], axis=-1, keepdims=True)
    key_sum = jnp.sum(raw[1] * raw[1], axis=-1, keepdims=True)
    packed = jnp.where(lane == 0, query_sum, jnp.where(lane == 1, key_sum, 0.0))
    squares[head] = jnp.transpose(packed)[0:8]

    def squares_to(target):
        return remote(squares.at[head], squares.at[head], s_send.at[target], s_recv.at[head], head=target)

    for j in range(1, 4):
        squares_to((head + j) % 4).start()
    product(2)
    for load in late:
        load.start()
    value[...] = raw[2].astype(BF16)
    angles = own_info[:, 1:2] * frequency_ref[...]
    cos_ref[...] = jnp.cos(angles)
    sines = jnp.sin(angles)
    sin_ref[...] = jnp.where(lane < HD // 2, -sines, sines)
    total = squares[head]
    for j in range(1, 4):
        source = (head + j) % 4
        remote(squares.at[source], squares.at[source], s_send.at[source], s_recv.at[source], head=source).wait_recv()
        total = total + squares[source]
    spread = jnp.transpose(jnp.concatenate([total] * (HD // 8), axis=0))
    scales = lax.rsqrt(spread / width + EPS)
    query_scale, key_scale = scales[:, 0:1], scales[:, 1:2]

    def turned(c, h, by):
        at = slice(h * HD, (h + 1) * HD)
        normed = raw[c, :, at] * by * gain_ref[c : c + 1, at]
        swapped = pltpu.roll(normed, HD // 2, 1)
        return (normed * cos_ref[...] + swapped * sin_ref[...]).astype(BF16)

    for h in range(heads):
        query[h] = turned(0, h, query_scale)

    def query_to(target):
        return remote(query.at[target], query_in.at[mine], q_send.at[target], q_recv.at[mine], blk=holder(target))

    for j in range(1, heads):
        query_to((mine + j) % heads).start()
    query_in[mine] = query[mine]
    for step in range(1, heads):
        pass_on(step)
    for h in range(heads):
        key[h] = turned(1, h, key_scale)

    row_at = lax.broadcasted_iota(jnp.int32, (rows, rows), 0)
    key_at = lax.broadcasted_iota(jnp.int32, (rows, rows), 1)
    see_leaf = (key_at.astype(F32) >= own_info[:, 0:1]) & (key_at <= row_at)
    over = (((1,), (1,)), ((), ()))
    def leaf_part(h):
        scores = lax.dot_general(query[h], key[h], over, preferred_element_type=F32) * scale
        scores = jnp.where(see_leaf, scores, NEG)
        top = jnp.max(scores, axis=-1, keepdims=True)
        weights = jnp.exp(scores - top)
        leaf_peak[h] = jnp.broadcast_to(top, (rows, HD))
        leaf_norm[h] = jnp.broadcast_to(jnp.sum(weights, axis=-1, keepdims=True), (rows, HD))
        leaf_acc[h] = jnp.dot(weights.astype(BF16), value[:, h * HD : (h + 1) * HD], preferred_element_type=F32)

    for h in range(heads // 2):
        leaf_part(h)

    for j in range(1, heads):
        source = (mine + j) % heads
        remote(query.at[0], query_in.at[source], q_send.at[0], q_recv.at[source], blk=holder(source)).wait_recv()
    key_row = lax.broadcasted_iota(jnp.int32, (rows, node_rows), 1).astype(F32)

    def part_to(target):
        return (
            remote(part_out.at[target], part_in.at[mine], p_send.at[target], p_recv.at[mine], blk=holder(target)),
            remote(stat_out.at[target], stat_in.at[mine], t_send.at[target], t_recv.at[mine], blk=holder(target)),
        )

    for copy in own_copies:
        copy.wait()
    for j in range(spread_count):
        member = (rest + j) % spread_count
        if j > 0:
            for step in range(heads):
                cache_wait(by_distance(mine, heads, step), member)

        @pl.loop(0, heads)
        def _(turn):
            g = (mine + 1 + turn) % heads
            scores = lax.dot_general(query_in[g], keys_in[member], over, preferred_element_type=F32) * scale
            limit = limits[g]
            masked = [
                jnp.where(
                    key_row < limit[:, j * heads + index : j * heads + index + 1],
                    scores[:, index * node_rows : (index + 1) * node_rows],
                    NEG,
                )
                for index in range(heads)
            ]
            highest = functools.reduce(jnp.maximum, masked)
            top = jnp.max(highest, axis=-1, keepdims=True)
            if j > 0:
                top = jnp.maximum(top, peak[g][:, 0:1])
            weights = [jnp.exp(part - top) for part in masked]
            total = jnp.sum(functools.reduce(jnp.add, weights), axis=-1, keepdims=True)
            summed = jnp.dot(
                jnp.concatenate([part.astype(BF16) for part in weights], axis=-1),
                values_in[member],
                preferred_element_type=F32,
            )
            if j > 0:
                shrink = jnp.exp(peak[g][:, 0:1] - top)
                total = total + norm[g][:, 0:1] * shrink
                summed = summed + acc[g] * shrink
            if j < spread_count - 1:
                peak[g] = jnp.broadcast_to(top, (rows, HD))
                norm[g] = jnp.broadcast_to(total, (rows, HD))
                acc[g] = summed
            else:
                part_out[g] = (summed / total).astype(BF16)
                stats = jnp.where(lane == 0, top, jnp.where(lane == 1, total, 0.0))
                stat_out[g] = jnp.transpose(stats)[0:8]

                @pl.when(turn < heads - 1)
                def _():
                    for copy in part_to(g):
                        copy.start()

    part_in[mine] = part_out[mine]
    stat_in[mine] = stat_out[mine]
    for h in range(heads // 2, heads):
        leaf_part(h)
    for j in range(1, heads):
        source = (mine + j) % heads
        remote(part_out.at[0], part_in.at[source], p_send.at[0], p_recv.at[source], blk=holder(source)).wait_recv()
        remote(stat_out.at[0], stat_in.at[source], t_send.at[0], t_recv.at[source], blk=holder(source)).wait_recv()
    for h in range(heads):
        stats = jnp.transpose(jnp.concatenate([stat_in[h]] * (HD // 8), axis=0))
        other_peak, other_norm = stats[:, 0:1], stats[:, 1:2]
        top = jnp.maximum(leaf_peak[h], other_peak)
        own_scale = jnp.exp(leaf_peak[h] - top)
        other_scale = jnp.exp(other_peak - top) * other_norm
        summed = leaf_acc[h] * own_scale + part_in[h].astype(F32) * other_scale
        attended[:, h * HD : (h + 1) * HD] = (
            summed / (leaf_norm[h] * own_scale + other_scale)
        ).astype(BF16)

    loads[3].wait()
    y, core = head // 2, head % 2
    own_rows = out_ref.shape[0]
    sibling, across = y * 2 + 1 - core, (1 - y) * 2 + core
    tiles = c_send.shape[1]
    wide = width // tiles

    def rows_of(index):
        return pl.ds(pl.multiple_of(index * own_rows, own_rows), own_rows)

    def cols_of(t):
        return pl.ds(t * wide, wide)

    def to_pair(half, t):
        return remote(
            proj_low.at[rows_of(half * 2 + 1 - core), cols_of(t)],
            pair_in.at[half, :, cols_of(t)],
            c_send.at[half, t], c_recv.at[half, t], head=sibling,
        )

    def to_line(t):
        return remote(pair_out.at[:, cols_of(t)], line_in.at[:, cols_of(t)], y_send.at[t], y_recv.at[t], head=across)

    def on_line(t):
        to_pair(1 - y, t).wait_recv()
        pair_out[:, cols_of(t)] = (
            proj[rows_of(across), cols_of(t)] + pair_in[1 - y, :, cols_of(t)].astype(F32)
        ).astype(BF16)
        to_line(t).start()

    for t in range(tiles):
        tiled = jnp.dot(attended[...], wout[:, cols_of(t)], preferred_element_type=F32)
        proj[:, cols_of(t)] = tiled
        proj_low[:, cols_of(t)] = tiled.astype(BF16)
        to_pair(1 - y, t).start()
        to_pair(y, t).start()
        if t > 0:
            on_line(t - 1)
    on_line(tiles - 1)
    for t in range(tiles):
        to_pair(y, t).wait_recv()
        to_line(t).wait_recv()
    total = proj[rows_of(head), :] + pair_in[y].astype(F32) + line_in[...].astype(F32)
    shrink = lax.rsqrt(jnp.mean(total * total, axis=-1, keepdims=True) + EPS)
    own = states_ref[rows_of(head), :].astype(F32)
    mid_ref[...] = (own + total * shrink * post_ref[0:1, :]).astype(BF16)

    mlp_part(
        lines, late,
        mid_ref, post_ref, out_ref,
        gathered, wgu, wd, hidden, whole, own_part, own_sum, send_x, recv_x, recv_z,
        g_send, g_recv, x_send, x_recv, z_send, z_recv,
    )

    for t in range(tiles):
        to_line(t).wait_send()
        for half in range(2):
            to_pair(half, t).wait_send()
    for j in range(1, 4):
        squares_to((head + j) % 4).wait_send()
    for j in range(1, heads):
        target = (mine + j) % heads
        query_to(target).wait_send()
        for copy in cache_out(target) + part_to(target):
            copy.wait_send()
    for source in range(heads):
        for j in range(1, spread_count):
            for copy in cache_on(source, j, False):
                copy.wait_send()


def on_device(
    states_in,
    w_qkv,
    qk_gain,
    w_out,
    post_gain,
    w_gate_up,
    w_down,
    cache_keys,
    cache_values,
    slot_node,
    node_length,
    node_parent,
    leaf_segment,
    leaf_node,
):
    rows, width = states_in.shape
    here = w_qkv.shape[2]
    heads = here // HD
    node_rows = cache_keys.shape[1]
    own_rows = rows // 4
    units = w_down.shape[0]
    slots = slot_node.shape[0]
    spread_count = slots // heads
    lines = slots // 2
    tiles = 4
    vmem = pl.BlockSpec(memory_space=pltpu.VMEM)
    smem = pl.BlockSpec(memory_space=pltpu.SMEM)
    hbm = pl.BlockSpec(memory_space=pl.ANY)
    dma = pltpu.SemaphoreType.DMA
    half = HD // 2
    frequency = (THETA ** (-2.0 * np.arange(half) / HD)).astype(np.float32)

    def per_head(kind):
        return pltpu.VMEM((heads, rows, HD), kind)

    cached = pltpu.VMEM((spread_count, heads * node_rows, HD), BF16)
    part = pltpu.VMEM((lines, own_rows, width), BF16)
    return pl.pallas_call(
        functools.partial(layer_kernel, spread_count),
        out_shape=jax.ShapeDtypeStruct((own_rows, width), BF16),
        in_specs=[vmem, hbm, vmem, hbm, vmem, hbm, hbm, hbm, hbm, smem, smem, smem, vmem, smem, vmem],
        out_specs=vmem,
        scratch_shapes=[
            pltpu.VMEM(w_qkv.shape, BF16),
            pltpu.VMEM(w_out.shape, BF16),
            pltpu.VMEM((3, rows, here), F32),
            per_head(BF16),
            per_head(BF16),
            pltpu.VMEM((rows, here), BF16),
            pltpu.VMEM((4, 8, rows), F32),
            per_head(BF16),
            cached,
            cached,
            pltpu.VMEM((rows, HD), F32),
            pltpu.VMEM((rows, HD), F32),
            per_head(F32),
            pltpu.VMEM((rows, HD), F32),
            per_head(F32), per_head(F32), per_head(F32),
            per_head(F32), per_head(F32), per_head(F32),
            per_head(BF16), per_head(BF16),
            pltpu.VMEM((heads, 8, rows), F32),
            pltpu.VMEM((heads, 8, rows), F32),
            pltpu.VMEM((rows, here), BF16),
            pltpu.VMEM((rows, width), F32),
            pltpu.VMEM((rows, width), BF16),
            pltpu.VMEM((2, own_rows, width), BF16),
            pltpu.VMEM((own_rows, width), BF16),
            pltpu.VMEM((own_rows, width), BF16),
            pltpu.VMEM((own_rows, width), BF16),
            pltpu.VMEM((slots * own_rows, width), BF16),
            pltpu.VMEM(w_gate_up.shape, BF16),
            pltpu.VMEM(w_down.shape, BF16),
            pltpu.VMEM((2 * own_rows, units), BF16),
            pltpu.VMEM((2 * own_rows, width), F32),
            pltpu.VMEM((2, own_rows, width), F32),
            pltpu.VMEM((own_rows, width), F32),
            part, part, part,
            dma((7,)),
            dma((4,)), dma((4,)),
            dma((heads,)), dma((heads,)),
            dma((2,)),
            dma((spread_count, heads)), dma((heads, spread_count)),
            dma((spread_count, heads)), dma((heads, spread_count)),
            dma((heads,)), dma((heads,)),
            dma((heads,)), dma((heads,)),
            dma((2, tiles)), dma((2, tiles)),
            dma((tiles,)), dma((tiles,)),
            dma((3, slots)),
            dma((slots,)),
            dma((lines, tiles)), dma((lines, tiles)),
            dma((lines, tiles)), dma((lines, tiles)),
        ],
        compiler_params=pltpu.CompilerParams(
            collective_id=1, has_side_effects=True, vmem_limit_bytes=62 * 2**20
        ),
    )(
        states_in, w_qkv, qk_gain, w_out, post_gain, w_gate_up, w_down, cache_keys, cache_values,
        slot_node, node_length, node_parent, leaf_segment, leaf_node,
        np.concatenate([frequency, frequency])[None, :],
    )


def solution(mesh):
    placed = (
        P("blk", None),
        P(None, None, "head"),
        P(None, "head"),
        P("head", None),
        P(),
        P(None, None, "blk"),
        P("blk", None),
        P("blk", None, "head"),
        P("blk", None, "head"),
        P(),
        P(),
        P(),
        P(),
        P(),
    )
    return jax.shard_map(
        on_device, mesh=mesh, in_specs=placed, out_specs=P(("blk", "head"), None), check_vma=False
    )
```
